128 devices in a mesh: dp: 4 (over y), tensor: 32 (over z, x, core).
Axes of the slice: x: 4, y: 4, z: 4, core: 2. Of those that a mesh axis runs over, the one named last changes fastest.
Arguments:
- prompt_states: bfloat16 [8, 512, 2048], P('dp', 'tensor')
- decode_states: bfloat16 [128, 2048], P(('dp', 'tensor'))
- cache: bfloat16 [2, 136, 1536, 2048], P(None, 'dp', 'tensor'), may hold values from -160 to 160
- prompt_starts: int32 [8], replicated, may hold values from 0 to 1536, as said below
- decode_lengths: int32 [128], replicated, may hold values from 1 to 1536, as said below
- decode_slots: int32 [128], replicated, may hold values from 0 to 127, each once
- w_qkv: bfloat16 [3, 2048, 2048], P(None, None, 'tensor')
- w_out: bfloat16 [2048, 2048], P('tensor')
- w_gate_up: bfloat16 [2, 2048, 8192], P(None, None, 'tensor')
- w_down: bfloat16 [8192, 2048], P('tensor')
- gains: float32 [4, 2048], replicated, may hold values from 0.25 to 1.75
Outputs:
- prompt_out: bfloat16 [8, 512, 2048], P('dp', 'tensor')
- decode_out: bfloat16 [128, 2048], P(('dp', 'tensor'))
- new_prompt_kv: bfloat16 [2, 8, 512, 2048], P(None, 'dp', 'tensor')
- new_decode_kv: bfloat16 [2, 128, 2048], P(None, ('dp', 'tensor'))
The draws below stay inside these ranges and needn't reach their ends.
Inputs may be any that keep to these rules, and one draw needn't show every extreme that they name: Decode request e sits in decode slot decode_slots[e]; each slot holds one request. `prompt_starts`: some prompt has exactly 1536 cached positions. `decode_lengths`: some decode request has exactly 1536 cached positions.
All inputs are finite; a program needn't handle non-finite values.
Results may differ from the reference program's by a relative error of at most 0.02.
Values may be sent and summed in bfloat16 or wider, within the bound.
A program may use at most 256 MiB of HBM per device.

```python
import jax
import jax.numpy as jnp
from jax import lax

D = 2048
HD = 128
FF = 8192
GROUP = 512
PRE_DEV = 2
DEC_DEV = 32
CTX_DEV = 48
SLOTS_DEV = 34
SLOTS = 136
PREFILLS = 8
DECODES = 128
CACHE = 1536
N_TENSOR = 32


def scaled_weight(key, full_shape, fan_in):
    key_base, key_scale = jax.random.split(key)
    column_shape = full_shape[:-2] + (1, full_shape[-1])
    base_values = jnp.clip(jax.random.normal(key_base, full_shape, jnp.float32), -6.0, 6.0)
    column_scale = jnp.exp(jax.random.uniform(key_scale, column_shape, jnp.float32, 0.0, 2.3025851))
    return base_values * column_scale * fan_in ** (-0.5) / 4.6


def scaled_rows(key, full_shape):
    key_base, key_scale = jax.random.split(key)
    row_shape = full_shape[:-1] + (1,)
    base_values = jnp.clip(jax.random.normal(key_base, full_shape, jnp.float32), -6.0, 6.0)
    row_scale = jnp.exp(jax.random.uniform(key_scale, row_shape, jnp.float32, -1.2039728, 1.0986123))
    return base_values * row_scale


def skewed_lengths(key, count, lowest):
    key_first, key_second, key_pick = jax.random.split(key, 3)
    first_draw = jax.random.randint(key_first, (count,), lowest, CACHE + 1)
    second_draw = jax.random.randint(key_second, (count,), lowest, CACHE + 1)
    chosen = jax.random.randint(key_pick, (), 0, count)
    lengths = jnp.minimum(first_draw, second_draw)
    return jnp.where(jnp.arange(count) == chosen, CACHE, lengths).astype(jnp.int32)


def draw_prompt_states(key, part):
    return scaled_rows(key, (PREFILLS, GROUP, D)).astype(jnp.bfloat16)


def draw_decode_states(key, part):
    return scaled_rows(key, (DECODES, D)).astype(jnp.bfloat16)


def draw_cache(key, part):
    key_keys, key_values = jax.random.split(key, 2)
    full_shape = (SLOTS, CACHE, D)
    stored_keys = jnp.clip(jax.random.normal(key_keys, full_shape, jnp.float32), -6.0, 6.0)
    stored_values = jnp.clip(jax.random.normal(key_values, full_shape, jnp.float32), -6.0, 6.0)
    return jnp.stack([stored_keys, stored_values]).astype(jnp.bfloat16)


def draw_prompt_starts(key, part):
    return skewed_lengths(key, PREFILLS, 0)


def draw_decode_lengths(key, part):
    return skewed_lengths(key, DECODES, 1)


def draw_w_qkv(key, part):
    return scaled_weight(key, (3, D, D), D).astype(jnp.bfloat16)


def draw_w_out(key, part):
    return scaled_weight(key, (D, D), D).astype(jnp.bfloat16)


def draw_w_gate_up(key, part):
    return scaled_weight(key, (2, D, FF), D).astype(jnp.bfloat16)


def draw_w_down(key, part):
    return scaled_weight(key, (FF, D), FF).astype(jnp.bfloat16)


def setup_inputs(seed: int = 0) -> dict:
    key_list = jax.random.split(jax.random.key(seed), 12)
    prompt_states = draw_prompt_states(jax.random.fold_in(key_list[11], 71), 0)
    decode_states = draw_decode_states(jax.random.fold_in(key_list[11], 71), 0)
    cache = draw_cache(jax.random.fold_in(key_list[11], 71), 0)
    prompt_starts = draw_prompt_starts(jax.random.fold_in(key_list[11], 71), 0)
    decode_lengths = draw_decode_lengths(jax.random.fold_in(key_list[11], 71), 0)
    decode_slots = jax.random.permutation(key_list[5], DECODES).astype(jnp.int32)
    w_qkv = draw_w_qkv(jax.random.fold_in(key_list[11], 71), 0)
    w_out = draw_w_out(jax.random.fold_in(key_list[11], 71), 0)
    w_gate_up = draw_w_gate_up(jax.random.fold_in(key_list[11], 71), 0)
    w_down = draw_w_down(jax.random.fold_in(key_list[11], 71), 0)
    gains = jnp.clip(1.0 + 0.15 * jax.random.normal(key_list[10], (4, D), jnp.float32), 0.25, 1.75)
    return {"prompt_states": prompt_states, "decode_states": decode_states, "cache": cache, "prompt_starts": prompt_starts, "decode_lengths": decode_lengths, "decode_slots": decode_slots, "w_qkv": w_qkv, "w_out": w_out, "w_gate_up": w_gate_up, "w_down": w_down, "gains": gains}


EPSILON = 1e-06
ROPE_BASE = 500000.0
MASKED_SCORE = -1e+30

def rms_scale(values, gain_vec):
    return values * lax.rsqrt(lax.optimization_barrier(jnp.mean(values * values, axis=-1, keepdims=True)) + EPSILON) * gain_vec

def rotate(values, positions):
    full_shape = values.shape
    paired = values.reshape(full_shape[:-1] + (full_shape[-1] // HD, HD // 2, 2))
    freq_index = jnp.arange(HD // 2, dtype=jnp.float32)
    inv_freq = jnp.power(ROPE_BASE, -2.0 * freq_index / HD)
    angles = positions.astype(jnp.float32)[..., None, None] * inv_freq
    cosine = jnp.cos(angles)
    sine_values = jnp.sin(angles)
    even_part = paired[..., 0]
    odd_part = paired[..., 1]
    turned = jnp.stack([even_part * cosine - odd_part * sine_values, even_part * sine_values + odd_part * cosine], axis=-1)
    return turned.reshape(full_shape)

def round_trip(values):
    rounded = lax.optimization_barrier(values.astype(jnp.bfloat16))
    return rounded.astype(jnp.float32)

def block_sum(operand, weights, blocks):
    row_count = operand.shape[0]
    inner_width = operand.shape[1] // blocks
    operands = jnp.transpose(operand.reshape(row_count, blocks, inner_width), (1, 0, 2))
    weight_blocks = weights.reshape(blocks, inner_width, weights.shape[1])

    def accumulate(running, couple):
        partial_value = jnp.dot(couple[0], couple[1], preferred_element_type=jnp.float32).astype(jnp.bfloat16)
        partial_value = lax.optimization_barrier(partial_value)
        return (running + partial_value.astype(jnp.float32), None)
    initial = jnp.zeros((row_count, weights.shape[1]), jnp.float32)
    running, unused = lax.scan(accumulate, initial, (operands, weight_blocks))
    return running

def reference(prompt_states, decode_states, cache, prompt_starts, decode_lengths, decode_slots, w_qkv, w_out, w_gate_up, w_down, gains):
    head_count = D // HD
    prompt_rows = PREFILLS * GROUP
    part_rows = GROUP // N_TENSOR
    states = jnp.concatenate([prompt_states.reshape(prompt_rows, D), decode_states], axis=0)
    projected = jnp.einsum('rd,kde->kre', states.astype(jnp.float32), w_qkv.astype(jnp.float32), precision=lax.Precision.HIGHEST)
    query_raw = projected[0].astype(jnp.bfloat16)
    key_raw = projected[1].astype(jnp.bfloat16)
    value_new = projected[2].astype(jnp.bfloat16)
    slot_request = jnp.zeros((DECODES,), jnp.int32).at[decode_slots].set(jnp.arange(DECODES, dtype=jnp.int32))
    slot_length = decode_lengths[slot_request]
    offsets = jnp.arange(GROUP, dtype=jnp.int32)
    prompt_pos = prompt_starts[:, None] + offsets[None, :]
    positions = jnp.concatenate([prompt_pos.reshape(prompt_rows), slot_length], axis=0)
    query_new = rotate(rms_scale(query_raw.astype(jnp.float32), gains[0]), positions).astype(jnp.bfloat16)
    key_new = rotate(rms_scale(key_raw.astype(jnp.float32), gains[1]), positions).astype(jnp.bfloat16)
    scale_factor = HD ** (-0.5)
    prompt_ids = jnp.arange(PREFILLS, dtype=jnp.int32)
    prompt_cache = prompt_ids // PRE_DEV * SLOTS_DEV + prompt_ids % PRE_DEV
    decode_ids = jnp.arange(DECODES, dtype=jnp.int32)
    decode_cache = decode_ids // DEC_DEV * SLOTS_DEV + PRE_DEV + decode_ids % DEC_DEV
    decode_block = decode_ids % DEC_DEV // (DEC_DEV // N_TENSOR)
    cache_pos = jnp.arange(CACHE, dtype=jnp.int32)
    block_ids = jnp.arange(N_TENSOR, dtype=jnp.int32)

    def prompt_block(inputs):
        slot_index, start_pos, queries, keys_in, values_in = inputs
        cached_keys = cache[0, slot_index].reshape(CACHE, head_count, HD).astype(jnp.float32)
        cached_values = cache[1, slot_index].reshape(N_TENSOR, CTX_DEV, head_count, HD).astype(jnp.float32)
        all_keys = jnp.concatenate([cached_keys, keys_in.reshape(GROUP, head_count, HD).astype(jnp.float32)], axis=0)
        fresh_values = values_in.reshape(N_TENSOR, part_rows, head_count, HD).astype(jnp.float32)
        query_heads = queries.reshape(GROUP, head_count, HD).astype(jnp.float32)
        scores = jnp.einsum('ihe,jhe->hij', query_heads, all_keys, precision=lax.Precision.HIGHEST) * scale_factor
        live_mask = jnp.concatenate([jnp.broadcast_to((cache_pos < start_pos)[None, :], (GROUP, CACHE)), offsets[None, :] <= offsets[:, None]], axis=1)
        scores = jnp.where(live_mask[None], scores, MASKED_SCORE)
        highest = lax.optimization_barrier(jnp.max(scores, axis=-1, keepdims=True))
        weights = jnp.where(live_mask[None], jnp.exp(scores - highest), 0.0)
        totals = lax.optimization_barrier(jnp.sum(weights, axis=-1))
        probs = round_trip(weights)
        cached_probs = probs[..., :CACHE].reshape(head_count, GROUP, N_TENSOR, CTX_DEV)
        fresh_probs = probs[..., CACHE:].reshape(head_count, GROUP, N_TENSOR, part_rows)
        partials = jnp.einsum('hitj,tjhe->tihe', cached_probs, cached_values, precision=lax.Precision.HIGHEST)
        partials = partials + jnp.einsum('hitj,tjhe->tihe', fresh_probs, fresh_values, precision=lax.Precision.HIGHEST)
        mixed_sum = lax.optimization_barrier(jnp.sum(round_trip(partials), axis=0))
        return (mixed_sum / jnp.transpose(totals)[:, :, None]).reshape(GROUP, D).astype(jnp.bfloat16)

    def decode_one(inputs):
        slot_index, length, owner_block, query_row, key_own, value_own = inputs
        cached_keys = cache[0, slot_index].reshape(CACHE, head_count, HD).astype(jnp.float32)
        cached_values = cache[1, slot_index].reshape(N_TENSOR, CTX_DEV, head_count, HD).astype(jnp.float32)
        query_heads = query_row.reshape(head_count, HD).astype(jnp.float32)
        cached_scores = jnp.einsum('he,jhe->hj', query_heads, cached_keys, precision=lax.Precision.HIGHEST) * scale_factor
        own_score = lax.optimization_barrier(jnp.sum(query_heads * key_own.reshape(head_count, HD).astype(jnp.float32), axis=-1)) * scale_factor
        live_mask = cache_pos < length
        cached_scores = jnp.where(live_mask[None], cached_scores, MASKED_SCORE)
        highest = jnp.maximum(lax.optimization_barrier(jnp.max(cached_scores, axis=-1)), own_score)
        cached_weights = jnp.where(live_mask[None], jnp.exp(cached_scores - highest[:, None]), 0.0)
        own_weight = jnp.exp(own_score - highest)
        totals = lax.optimization_barrier(jnp.sum(cached_weights, axis=-1)) + own_weight
        cached_probs = round_trip(cached_weights).reshape(head_count, N_TENSOR, CTX_DEV)
        own_prob = round_trip(own_weight)
        partials = jnp.einsum('htj,tjhe->the', cached_probs, cached_values, precision=lax.Precision.HIGHEST)
        own_term = own_prob[:, None] * value_own.reshape(head_count, HD).astype(jnp.float32)
        pick = jnp.where(block_ids == owner_block, 1.0, 0.0).astype(jnp.float32)
        partials = partials + pick[:, None, None] * own_term[None]
        mixed_sum = lax.optimization_barrier(jnp.sum(round_trip(partials), axis=0))
        return (mixed_sum / totals[:, None]).reshape(D).astype(jnp.bfloat16)
    prompt_attn = lax.map(prompt_block, (prompt_cache, prompt_starts, query_new[:prompt_rows].reshape(PREFILLS, GROUP, D), key_new[:prompt_rows].reshape(PREFILLS, GROUP, D), value_new[:prompt_rows].reshape(PREFILLS, GROUP, D)))
    decode_attn = lax.map(decode_one, (decode_cache, slot_length, decode_block, query_new[prompt_rows:], key_new[prompt_rows:], value_new[prompt_rows:]))
    attended = jnp.concatenate([prompt_attn.reshape(prompt_rows, D), decode_attn], axis=0)
    attn_sum = block_sum(attended, w_out, N_TENSOR)
    hidden = (states.astype(jnp.float32) + rms_scale(attn_sum, gains[2])).astype(jnp.bfloat16)
    gate_up = jnp.einsum('rd,kdf->krf', hidden.astype(jnp.float32), w_gate_up.astype(jnp.float32), precision=lax.Precision.HIGHEST)
    activated = (jax.nn.silu(gate_up[0]) * gate_up[1]).astype(jnp.bfloat16)
    ffn_sum = block_sum(activated, w_down, N_TENSOR)
    output = (hidden.astype(jnp.float32) + rms_scale(ffn_sum, gains[3])).astype(jnp.bfloat16)
    prompt_out = output[:prompt_rows].reshape(PREFILLS, GROUP, D)
    decode_out = output[prompt_rows:][decode_slots]
    new_prompt_kv = jnp.stack([key_new[:prompt_rows], value_new[:prompt_rows]]).reshape(2, PREFILLS, GROUP, D)
    new_decode_kv = jnp.stack([key_new[prompt_rows:], value_new[prompt_rows:]])
    return (prompt_out, decode_out, new_prompt_kv, new_decode_kv)
```

```python
import jax
import jax.numpy as jnp
import numpy as np
from jax import lax
from jax.experimental import pallas as pl
from jax.experimental.pallas import tpu as pltpu
from jax.sharding import PartitionSpec as P

D = 2048
HD = 128
HEADS = 16
FFD = 256
CTX = 48
ROWS = 528
EPSILON = 1e-06
ROPE_BASE = 500000.0
MASKED_SCORE = -1e30
SCALE = HD ** (-0.5)
BF = jnp.bfloat16
F32 = jnp.float32
MESH = pl.DeviceIdType.MESH
NT = (((1,), (1,)), ((), ()))


def mul(value, factor):
    return pl.multiple_of(value * factor, factor)


def remote(src, dst, send_sem, recv_sem, dev):
    return pltpu.make_async_remote_copy(
        src_ref=src,
        dst_ref=dst,
        send_sem=send_sem,
        recv_sem=recv_sem,
        device_id={"tensor": dev},
        device_id_type=MESH,
    )


class Plane:
    def __init__(self):
        self.y = lax.axis_index("dp")
        self.t = lax.axis_index("tensor")
        self.c = lax.rem(self.t, 2)
        self.q = lax.div(self.t, 2)
        x = lax.rem(self.q, 4)
        z = lax.div(self.q, 4)
        self.a = x + self.c * (z - x)
        self.b = z + self.c * (x - z)
        self.sib = self.t + 1 - 2 * self.c
        self.aR, self.aO, self.aL = [lax.rem(self.a + i, 4) for i in (1, 2, 3)]
        self.bR, self.bO, self.bL = [lax.rem(self.b + i, 4) for i in (1, 2, 3)]

    def chip(self, a, b):
        return a * (1 + 3 * self.c) + b * (4 - 3 * self.c)

    def dev(self, a, b):
        return 2 * self.chip(a, b) + self.c


def block(buf, chip):
    return buf.at[pl.ds(mul(chip, 32), 32)]


def half(buf, chip, h):
    return buf.at[pl.ds(mul(chip * 2 + h, 16), 16)]


def gather_steps(p, buf, ss, rs, sends):
    def send(slot, ref, dev):
        copy = remote(ref, ref, ss.at[slot], rs.at[slot], dev)
        copy.start()
        sends.append(copy)

    def recv(slot, ref):
        remote(ref, ref, ss.at[slot], rs.at[slot], p.dev(p.aR, p.b)).wait_recv()

    def blk(a, b):
        return block(buf, p.chip(a, b))

    def hlf(a, b, h):
        return half(buf, p.chip(a, b), h)

    a, b, aR, aL, aO, bR, bL, bO = p.a, p.b, p.aR, p.aL, p.aO, p.bR, p.bL, p.bO
    to_aR, to_aL, to_bR, to_bL = p.dev(aR, b), p.dev(aL, b), p.dev(a, bR), p.dev(a, bL)
    own = blk(a, b)
    send(0, own, to_aR)
    send(1, own, to_aL)
    send(4, own, to_bR)
    send(5, own, to_bL)
    yield
    recv(0, blk(aL, b))
    send(2, hlf(aL, b, 0), to_aR)
    send(8, blk(aL, b), to_bR)
    send(9, blk(aL, b), to_bL)
    recv(1, blk(aR, b))
    send(3, hlf(aR, b, 1), to_aL)
    send(12, blk(aR, b), to_bR)
    send(13, blk(aR, b), to_bL)
    yield
    recv(4, blk(a, bL))
    send(6, hlf(a, bL, 0), to_bR)
    recv(5, blk(a, bR))
    send(7, hlf(a, bR, 1), to_bL)
    yield
    recv(2, hlf(aO, b, 0))
    recv(3, hlf(aO, b, 1))
    send(16, blk(aO, b), to_bR)
    send(17, blk(aO, b), to_bL)
    yield
    for k, ak in ((1, aL), (2, aR), (3, aO)):
        recv(4 + 4 * k, blk(ak, bL))
        send(6 + 4 * k, hlf(ak, bL, 0), to_bR)
        recv(5 + 4 * k, blk(ak, bR))
        send(7 + 4 * k, hlf(ak, bR, 1), to_bL)
        yield
    for k, ak in ((0, a), (1, aL), (2, aR), (3, aO)):
        recv(6 + 4 * k, hlf(ak, bO, 0))
        recv(7 + 4 * k, hlf(ak, bO, 1))
        yield


def reduce_rows(p, buf, land, ss, rs, sends):
    def send(slot, ref, dev):
        copy = remote(ref, land.at[slot], ss.at[slot], rs.at[slot], dev)
        copy.start()
        sends.append(copy)

    def recv(slot):
        remote(land.at[slot], land.at[slot], ss.at[slot], rs.at[slot], p.dev(p.aR, p.b)).wait_recv()
        return land[slot].astype(F32)

    def hlf(a, b, h):
        return half(buf, p.chip(a, b), h)

    def add(ref, slots):
        total = ref[...].astype(F32)
        for slot in slots:
            total = total + recv(slot)
        return total

    a, b, aR, aL, aO, bR, bL, bO = p.a, p.b, p.aR, p.aL, p.aO, p.bR, p.bL, p.bO
    to_aR, to_aL, to_bR, to_bL = p.dev(aR, b), p.dev(aL, b), p.dev(a, bR), p.dev(a, bL)
    order = ((3, aO), (1, aL), (2, aR), (0, a))
    for k, ak in order:
        send(6 * k + 0, hlf(ak, bO, 0), to_bL)
        send(6 * k + 1, hlf(ak, bO, 1), to_bR)
        send(6 * k + 2, hlf(ak, bL, 1), to_bL)
        send(6 * k + 3, hlf(ak, bR, 0), to_bR)
    for k, ak in order:
        ref = hlf(ak, bL, 0)
        ref[...] = add(ref, (6 * k + 0,)).astype(BF)
        send(6 * k + 4, ref, to_bL)
        ref = hlf(ak, bR, 1)
        ref[...] = add(ref, (6 * k + 1,)).astype(BF)
        send(6 * k + 5, ref, to_bR)
    for k, ak in order:
        h0, h1 = hlf(ak, b, 0), hlf(ak, b, 1)
        h0[...] = add(h0, (6 * k + 3, 6 * k + 4)).astype(BF)
        h1[...] = add(h1, (6 * k + 2, 6 * k + 5)).astype(BF)
        if k == 3:
            send(24, h0, to_aL)
            send(25, h1, to_aR)
        if k == 1:
            send(26, h1, to_aL)
        if k == 2:
            send(27, h0, to_aR)
    ref = hlf(aL, b, 0)
    ref[...] = add(ref, (24,)).astype(BF)
    send(28, ref, to_aL)
    ref = hlf(aR, b, 1)
    ref[...] = add(ref, (25,)).astype(BF)
    send(29, ref, to_aR)
    first = add(hlf(a, b, 0), (27, 28))
    second = add(hlf(a, b, 1), (26, 29))
    return jnp.concatenate([first, second], axis=0)


def turn(values, cosine, sine):
    lane = lax.broadcasted_iota(jnp.int32, values.shape, 1)
    swapped = jnp.where(lane % 2 == 0, pltpu.roll(values, HD - 1, 1), pltpu.roll(values, 1, 1))
    return values * cosine + swapped * sine


def angles(positions, freq):
    turned = positions * freq
    lane = lax.broadcasted_iota(jnp.int32, turned.shape, 1)
    return jnp.cos(turned), jnp.where(lane % 2 == 0, -1.0, 1.0) * jnp.sin(turned)


def kernel(
    prompt_states,
    decode_states,
    cache,
    prompt_starts,
    lengths,
    slots_row,
    slots,
    w_qkv,
    w_out,
    w_gate_up,
    w_down,
    gains,
    freq,
    prompt_out,
    decode_out,
    new_prompt_kv,
    new_decode_kv,
    X1,
    X2,
    Y,
    Y2,
    RB1,
    RB2,
    WQ,
    WO,
    WG,
    WD,
    KD,
    VD,
    CK,
    QR,
    KN,
    NKV,
    ATT,
    ACT,
    SS,
    DX,
    XD,
    DQ,
    DKV,
    QH,
    KH,
    LEN,
    DCS,
    OBF,
    OB,
    SB,
    OR,
    SR,
    DY,
    DR,
    DX2,
    DY2,
    DR2,
    PO,
    FIN,
    FS,
    FD,
    g1s,
    g1r,
    g2s,
    g2r,
    r1s,
    r1r,
    r2s,
    r2r,
    ws,
    wr,
    wl,
    ls,
    ms,
    mr,
    ys,
    yr,
):
    p = Plane()
    y, t, c, q, sib = p.y, p.t, p.c, p.q, p.sib
    sends = []
    lanes_q = pl.ds(mul(q, HD), HD)

    barrier = pltpu.get_barrier_semaphore()

    @pl.loop(1, 32)
    def _(i):
        pl.semaphore_signal(
            barrier, inc=1, device_id={"tensor": lax.rem(t + i, 32)}, device_id_type=MESH
        )

    for i in (1, 2, 3):
        pl.semaphore_signal(barrier, inc=1, device_id={"dp": lax.rem(y + i, 4)}, device_id_type=MESH)
    pl.semaphore_wait(barrier, 34)

    def plane_peers(body):
        @pl.loop(1, 16)
        def _(i):
            chip = lax.rem(q + i, 16)
            body(chip, 2 * chip + c)

    def group_peers(body):
        @pl.loop(1, 32)
        def _(i):
            body(lax.rem(t + i, 32))

    def drain_recv(ref, sem):
        remote(ref, ref, sem, sem, sib).wait_recv()

    def drain_send(ref, sem):
        remote(ref, ref, sem, sem, sib).wait_send()

    for j in range(HEADS):
        DX[q, pl.ds(j, 1), :] = decode_states[:, j * HD : (j + 1) * HD].astype(F32)
    plane_peers(lambda chip, dev: remote(DX.at[q], DX.at[q], ms.at[0], mr.at[0], dev).start())

    piece = remote(
        prompt_states.at[1 - c], half(X1, q, c), ws.at[0], wr.at[0], sib
    )
    piece.start()
    piece_here = pltpu.make_async_copy(prompt_states.at[c], half(X1, q, c), wl.at[0])
    piece_here.start()
    weights = []
    for i, (src, dst) in enumerate(
        (
            (w_qkv, WQ.at[:, c]),
            (w_out, WO.at[c]),
            (w_gate_up, WG.at[c]),
            (w_down, WD.at[c]),
        )
    ):
        here = pltpu.make_async_copy(src, dst, wl.at[1 + i])
        there = remote(src, dst, ws.at[1 + i], wr.at[1 + i], sib)
        here.start()
        there.start()
        weights.append((here, there))

    def weight_here(i):
        here, there = weights[i]
        here.wait()
        there.wait_recv()

    loads = []
    for i, (kv, dst) in enumerate(((0, KD), (1, VD))):
        for part in range(2):
            load = pltpu.make_async_copy(
                cache.at[kv, pl.ds(2 + 16 * part, 16)], dst.at[pl.ds(16 * part, 16)], ls.at[2 * i + part]
            )
            load.start()
            loads.append(load)

    piece_here.wait()
    piece.wait_recv()
    steps = gather_steps(p, X1, g1s, g1r, sends)
    next(steps)

    def cache_slice(dev):
        return cache.at[:, lax.rem(dev, 2), :, pl.ds(mul(lax.div(dev, 2), HD), HD)]

    own_cache = pltpu.make_async_copy(cache_slice(t), CK.at[:, t], wl.at[5])
    own_cache.start()
    group_peers(
        lambda dev: remote(cache_slice(dev), CK.at[:, t], ms.at[1], mr.at[1], dev).start()
    )

    drain_recv(DX.at[pl.ds(0, 15)], mr.at[0])
    for j in range(HEADS):
        XD[:, j * HD : (j + 1) * HD] = DX[:, j, :].astype(BF)
    weight_here(0)

    def project(rows):
        return lax.dot_general(rows, WQ[...].reshape(3 * HD, D), NT, preferred_element_type=F32)

    dec = project(XD[...]).astype(BF)
    DQ[c, :, lanes_q] = dec[:, :HD]
    DKV[0, :, lanes_q] = dec[:, HD : 2 * HD]
    DKV[1, :, lanes_q] = dec[:, 2 * HD :]
    q_own = DQ.at[c, :, lanes_q]
    kv_own = DKV.at[:, :, lanes_q]
    group_peers(lambda dev: remote(q_own, q_own, ms.at[2], mr.at[2], dev).start())
    plane_peers(lambda chip, dev: remote(kv_own, kv_own, ms.at[3], mr.at[3], dev).start())
    next(steps)

    slot_row = lax.broadcasted_iota(jnp.int32, (32, HD), 0)
    slot_id = 32 * y + 2 * (slot_row % 16) + slot_row // 16
    matched = jnp.where(slots_row[...] == slot_id, lengths[...].astype(F32), 0.0)
    slot_len = jnp.sum(matched, axis=1, keepdims=True)
    LEN[...] = jnp.broadcast_to(slot_len, (32, HD))
    cosine, sine = angles(LEN[...], freq[...])
    DCS[0] = cosine
    DCS[1] = sine
    next(steps)

    drain_recv(OR.at[pl.ds(0, 31)], mr.at[2])
    drain_recv(KN.at[:, pl.ds(0, 240)], mr.at[3])

    def normed(raw, gain_row, first):
        scale = lax.rsqrt(jnp.mean(raw * raw, axis=1, keepdims=True) + EPSILON)
        rows = raw.shape[0]
        cos_part, sin_part = DCS[0, pl.ds(first, rows), :], DCS[1, pl.ds(first, rows), :]
        parts = []
        for j in range(HEADS):
            lanes = slice(j * HD, (j + 1) * HD)
            scaled = raw[:, lanes] * scale * gains[gain_row : gain_row + 1, lanes]
            parts.append(turn(scaled, cos_part, sin_part).astype(BF).astype(F32))
        return parts

    for plane in range(2):
        for j, part in enumerate(normed(DQ[plane].astype(F32), 0, 16 * plane)):
            QH[16 * plane : 16 * plane + 16, j * HD : (j + 1) * HD] = part
    for j, part in enumerate(normed(DKV[0].astype(F32), 1, mul(c, 16))):
        KH[:, j * HD : (j + 1) * HD] = part
    for load in loads:
        load.wait()

    own_lane = lax.broadcasted_iota(jnp.int32, (HEADS, D), 1) // HD
    own_row = lax.broadcasted_iota(jnp.int32, (HEADS, D), 0)
    own_head = own_lane == own_row
    spot = (lax.broadcasted_iota(jnp.int32, (HEADS, CTX), 1) + CTX * t).astype(F32)
    low_lane = lax.broadcasted_iota(jnp.int32, (HEADS, HD), 1) < 64

    def decode_slots_from(first, count):
        @pl.loop(first, first + count)
        def _(s):
            plane = lax.rem(s, 2)
            r = lax.div(s, 2)
            index = 16 * plane + r
            spread = jnp.where(own_head, QH[pl.ds(index, 1), :], 0.0).astype(BF)
            scores = lax.dot_general(spread, KD[s], NT, preferred_element_type=F32) * SCALE
            live = spot < LEN[pl.ds(index, 1), :CTX]
            scores = jnp.where(live, scores, MASKED_SCORE)
            top = jnp.max(scores, axis=1, keepdims=True)
            probs = jnp.where(live, jnp.exp(scores - top), 0.0)
            total = jnp.sum(probs, axis=1, keepdims=True)
            mixed = jnp.dot(probs.astype(BF), VD[s], preferred_element_type=F32)
            OBF[pl.ds(index, 1), :] = jnp.sum(jnp.where(own_head, mixed, 0.0), axis=0, keepdims=True)
            SB[plane, :, r, :] = jnp.where(low_lane, top, total)

    done = 0
    for _ in steps:
        if done < 32:
            decode_slots_from(done, 4)
            done += 4
    if done < 32:
        decode_slots_from(done, 32 - done)

    OB[0] = OBF[0:16, :].astype(BF)
    OB[1] = OBF[16:32, :].astype(BF)

    def mixed_slice(dev):
        return OB.at[lax.rem(dev, 2), :, pl.ds(mul(lax.div(dev, 2), HD), HD)]

    def stat_slice(dev):
        return SB.at[lax.rem(dev, 2), lax.div(dev, 2)]

    own_mixed = pltpu.make_async_copy(mixed_slice(t), OR.at[t], wl.at[6])
    own_stat = pltpu.make_async_copy(stat_slice(t), SR.at[t], wl.at[7])
    own_mixed.start()
    own_stat.start()

    def send_partial(dev):
        remote(mixed_slice(dev), OR.at[t], ms.at[4], mr.at[4], dev).start()
        remote(stat_slice(dev), SR.at[t], ms.at[5], mr.at[5], dev).start()

    group_peers(send_partial)

    stat_row = lax.broadcasted_iota(jnp.int32, (8, HD), 0)
    SS[q] = jnp.zeros((8, HD), F32)

    def row_sums(values):
        total = jnp.sum(values * values, axis=1, keepdims=True)
        return jnp.broadcast_to(total, (HD, HD)).T[0:8, :]

    @pl.loop(0, 4)
    def _(i):
        rows = pl.ds(mul(i, HD), HD)
        got = project(X1[rows, :])
        query = got[:, :HD].astype(BF)
        key = got[:, HD : 2 * HD].astype(BF)
        QR[rows, :] = query
        KN[0, rows, :] = key
        KN[1, rows, :] = got[:, 2 * HD :].astype(BF)
        query_sum = row_sums(query.astype(F32))
        key_sum = row_sums(key.astype(F32))
        SS[q] = jnp.where(
            stat_row == i, query_sum, jnp.where(stat_row == 4 + i, key_sum, SS[q])
        )

    plane_peers(lambda chip, dev: remote(SS.at[q], SS.at[q], ms.at[6], mr.at[6], dev).start())
    drain_recv(SS.at[pl.ds(0, 15)], mr.at[6])
    sums = jnp.sum(SS[...], axis=0)
    scales = lax.rsqrt(sums * (1.0 / D) + EPSILON)
    start = prompt_starts[2 * y + c]

    for i in range(4):
        rows = slice(i * HD, (i + 1) * HD)
        offset = lax.broadcasted_iota(jnp.int32, (HD, HD), 0) + i * HD
        cosine, sine = angles((offset + start).astype(F32), freq[...])
        for kind in range(2):
            column = jnp.broadcast_to(scales[4 * kind + i : 4 * kind + i + 1, :], (HD, HD)).T
            raw = (QR[rows, :] if kind == 0 else KN[0, rows, :]).astype(F32)
            turned = turn(raw * column * gains[kind : kind + 1, lanes_q], cosine, sine).astype(BF)
            if kind == 0:
                QR[rows, :] = turned
            else:
                KN[0, rows, :] = turned

    def fresh_slice(dev):
        return KN.at[:, pl.ds(mul(dev, 16), 16), :]

    landing = NKV.at[:, c, :, lanes_q]
    own_fresh = pltpu.make_async_copy(fresh_slice(t), landing, wl.at[8])
    own_fresh.start()
    group_peers(lambda dev: remote(fresh_slice(dev), landing, ms.at[7], mr.at[7], dev).start())

    own_cache.wait()
    drain_recv(CK.at[:, pl.ds(0, 31)], mr.at[1])

    @pl.loop(0, 4)
    def _(i):
        rows = pl.ds(mul(i, HD), HD)
        query = QR[rows, :]
        cached_keys = CK[0].reshape(32 * CTX, HD)
        cached_values = CK[1].reshape(32 * CTX, HD)
        fresh = lax.dot_general(query, KN[0], NT, preferred_element_type=F32) * SCALE
        cached = lax.dot_general(query, cached_keys, NT, preferred_element_type=F32) * SCALE
        column = lax.broadcasted_iota(jnp.int32, fresh.shape, 1)
        row = lax.broadcasted_iota(jnp.int32, fresh.shape, 0) + i * HD
        fresh_live = column <= row
        cached_live = lax.broadcasted_iota(jnp.int32, cached.shape, 1) < start
        fresh = jnp.where(fresh_live, fresh, MASKED_SCORE)
        cached = jnp.where(cached_live, cached, MASKED_SCORE)
        top = jnp.maximum(
            jnp.max(fresh, axis=1, keepdims=True), jnp.max(cached, axis=1, keepdims=True)
        )
        fresh = jnp.where(fresh_live, jnp.exp(fresh - top), 0.0)
        cached = jnp.where(cached_live, jnp.exp(cached - top), 0.0)
        total = jnp.sum(fresh, axis=1, keepdims=True) + jnp.sum(cached, axis=1, keepdims=True)
        mixed = jnp.dot(fresh.astype(BF), KN[1], preferred_element_type=F32)
        mixed = mixed + jnp.dot(cached.astype(BF), cached_values, preferred_element_type=F32)
        ATT[rows, :] = (mixed / total).astype(BF)

    own_mixed.wait()
    own_stat.wait()
    drain_recv(OR.at[pl.ds(0, 31)], mr.at[4])
    drain_recv(SR.at[pl.ds(0, 31)], mr.at[5])
    stats = SR[...].reshape(32 * 16, HD)
    rolled = pltpu.roll(stats, 64, 1)
    low = lax.broadcasted_iota(jnp.int32, stats.shape, 1) < 64
    tops = jnp.where(low, stats, rolled).reshape(32, 16, HD)
    totals = jnp.where(low, rolled, stats).reshape(32, 16, HD)
    own_rows = pl.ds(mul(c, 16), 16)
    own_score = (
        jnp.sum(QH[own_rows, lanes_q] * KH[:, lanes_q], axis=1, keepdims=True) * SCALE
    )
    highest = jnp.maximum(jnp.max(tops, axis=0), own_score)
    factors = jnp.exp(tops - highest[None])
    own_weight = jnp.exp(own_score - highest)
    total = jnp.sum(totals * factors, axis=0) + own_weight
    mixed = jnp.sum(OR[...].astype(F32) * factors, axis=0)
    mixed = mixed + own_weight.astype(BF).astype(F32) * DKV[1, :, lanes_q].astype(F32)
    ATT[512:528, :] = (mixed / total).astype(BF)

    weight_here(1)

    @pl.loop(0, 3)
    def _(i):
        rows = pl.ds(mul(i, 176), 176)
        Y[rows, :] = jnp.dot(
            ATT[rows, :], WO[...].reshape(HD, D), preferred_element_type=F32
        ).astype(BF)

    def spread_decode(source, staged, landed, index):
        tail = source[512:528, :].astype(F32)
        for j in range(HEADS):
            staged[:, j, :] = tail[:, j * HD : (j + 1) * HD]
        landed[q] = staged[q]
        plane_peers(
            lambda chip, dev: remote(
                staged.at[chip], landed.at[q], ms.at[index], mr.at[index], dev
            ).start()
        )

    def row_of(gain):
        parts = [gains[gain : gain + 1, j * HD : (j + 1) * HD] for j in range(HEADS)]
        return jnp.concatenate(parts, axis=0)

    def add_normed_rows(base, total, gain):
        scale = lax.rsqrt(jnp.mean(total * total, axis=1, keepdims=True) + EPSILON)
        return (base + total * scale * gains[gain : gain + 1, :]).astype(BF)

    def add_normed_row(base, total, gain):
        square = jnp.sum(total * total, axis=1, keepdims=True)
        mean = jnp.sum(square, axis=0, keepdims=True) * (1.0 / D)
        return (base + total * lax.rsqrt(mean + EPSILON) * row_of(gain)).astype(BF).astype(F32)

    own_block = pl.ds(mul(q, 32), 32)
    spread_decode(Y, DY, DR, 8)
    attn_rows = reduce_rows(p, Y, RB1, r1s, r1r, sends)
    X2[own_block, :] = add_normed_rows(X1[own_block, :].astype(F32), attn_rows, 2)
    steps = gather_steps(p, X2, g2s, g2r, sends)
    next(steps)
    drain_recv(DR.at[pl.ds(0, 15)], mr.at[8])
    DX2[q] = add_normed_row(DX[q], jnp.sum(DR[...], axis=0), 2)
    plane_peers(lambda chip, dev: remote(DX2.at[q], DX2.at[q], ms.at[9], mr.at[9], dev).start())
    for _ in steps:
        pass
    drain_recv(DX2.at[pl.ds(0, 15)], mr.at[9])
    for j in range(HEADS):
        X2[512:528, j * HD : (j + 1) * HD] = DX2[:, j, :].astype(BF)

    weight_here(2)
    weight_here(3)

    @pl.loop(0, 3)
    def _(i):
        rows = pl.ds(mul(i, 176), 176)
        hidden = X2[rows, :]
        for core in range(2):
            gate = jnp.dot(hidden, WG[core, 0], preferred_element_type=F32)
            up = jnp.dot(hidden, WG[core, 1], preferred_element_type=F32)
            ACT[core] = (gate / (1.0 + jnp.exp(-gate)) * up).astype(BF)
        Y2[rows, :] = (
            jnp.dot(ACT[0], WD[0], preferred_element_type=F32)
            + jnp.dot(ACT[1], WD[1], preferred_element_type=F32)
        ).astype(BF)

    spread_decode(Y2, DY2, DR2, 10)
    ffn_rows = reduce_rows(p, Y2, RB2, r2s, r2r, sends)
    out_rows = add_normed_rows(X2[own_block, :].astype(F32), ffn_rows, 3)
    FS[...] = out_rows.reshape(2, 16, D)
    PO[c] = FS[c]
    swap = remote(FS.at[1 - c], PO.at[c], ws.at[5], wr.at[5], sib)
    swap.start()

    drain_recv(DR2.at[pl.ds(0, 15)], mr.at[10])
    FIN[t] = add_normed_row(DX2[q], jnp.sum(DR2[...], axis=0), 3)
    group_peers(lambda dev: remote(FIN.at[t], FIN.at[t], ms.at[11], mr.at[11], dev).start())

    own_fresh.wait()
    drain_recv(KN.at[:, pl.ds(0, 496)], mr.at[7])
    new_prompt_kv[...] = NKV[...]
    mine = lax.broadcasted_iota(jnp.int32, (16, D), 0) == q
    new_decode_kv[0] = jnp.sum(jnp.where(mine, KH[...], 0.0), axis=0, keepdims=True).astype(BF)
    new_decode_kv[1] = jnp.sum(
        jnp.where(mine, DKV[1].astype(F32), 0.0), axis=0, keepdims=True
    ).astype(BF)

    drain_recv(FIN.at[pl.ds(0, 31)], mr.at[11])
    slot_of = lax.broadcasted_iota(jnp.int32, (32, 16, HD), 0) + 32 * y

    def wanted_row(yy):
        wanted = slots[32 * yy + t]
        return jnp.sum(jnp.where(slot_of == wanted, FIN[...], 0.0), axis=0)

    FD[0] = wanted_row(y)
    crossing = []
    for i in (1, 2, 3):
        other = lax.rem(y + i, 4)
        FD[3 + i] = wanted_row(other)
        copy = pltpu.make_async_remote_copy(
            src_ref=FD.at[3 + i],
            dst_ref=FD.at[i],
            send_sem=ys.at[i - 1],
            recv_sem=yr.at[i - 1],
            device_id={"dp": other},
            device_id_type=MESH,
        )
        copy.start()
        crossing.append(copy)
    swap.wait_recv()
    prompt_out[...] = PO[...]
    result = FD[0]
    for i, copy in enumerate(crossing):
        copy.wait_recv()
        result = result + FD[1 + i]
    for j in range(HEADS):
        decode_out[:, j * HD : (j + 1) * HD] = result[j : j + 1, :].astype(BF)

    for copy in sends + crossing + [piece, swap]:
        copy.wait_send()
    for _, there in weights:
        there.wait_send()
    drain_send(DX.at[pl.ds(0, 15)], ms.at[0])
    drain_send(CK.at[:, pl.ds(0, 31)], ms.at[1])
    drain_send(OR.at[pl.ds(0, 31)], ms.at[2])
    drain_send(KN.at[:, pl.ds(0, 240)], ms.at[3])
    drain_send(OR.at[pl.ds(0, 31)], ms.at[4])
    drain_send(SR.at[pl.ds(0, 31)], ms.at[5])
    drain_send(SS.at[pl.ds(0, 15)], ms.at[6])
    drain_send(KN.at[:, pl.ds(0, 496)], ms.at[7])
    drain_send(DR.at[pl.ds(0, 15)], ms.at[8])
    drain_send(DX2.at[pl.ds(0, 15)], ms.at[9])
    drain_send(DR2.at[pl.ds(0, 15)], ms.at[10])
    drain_send(FIN.at[pl.ds(0, 31)], ms.at[11])


def local(
    prompt_states,
    decode_states,
    cache,
    prompt_starts,
    decode_lengths,
    decode_slots,
    w_qkv,
    w_out,
    w_gate_up,
    w_down,
    gains,
):
    freq = np.power(ROPE_BASE, -2.0 * (np.arange(HD) // 2) / HD).astype(np.float32)[None, :]
    vmem = pl.BlockSpec(memory_space=pltpu.VMEM)
    smem = pl.BlockSpec(memory_space=pltpu.SMEM)
    hbm = pl.BlockSpec(memory_space=pl.ANY)
    scratch = [
        ((ROWS, D), BF),
        ((ROWS, D), BF),
        ((ROWS, D), BF),
        ((ROWS, D), BF),
        ((30, 16, D), BF),
        ((30, 16, D), BF),
        ((3, 2, 64, D), BF),
        ((2, 64, D), BF),
        ((2, 2, D, FFD), BF),
        ((2, FFD, D), BF),
        ((32, CTX, D), BF),
        ((32, CTX, D), BF),
        ((2, 32, CTX, HD), BF),
        ((512, HD), BF),
        ((2, 512, HD), BF),
        ((2, 2, 16, D), BF),
        ((ROWS, HD), BF),
        ((2, 176, FFD), BF),
        ((16, 8, HD), F32),
        ((16, 16, HD), F32),
        ((16, D), BF),
        ((2, 16, D), BF),
        ((2, 16, D), BF),
        ((32, D), F32),
        ((16, D), F32),
        ((32, HD), F32),
        ((2, 32, HD), F32),
        ((32, D), F32),
        ((2, 16, D), BF),
        ((2, 16, 16, HD), F32),
        ((32, 16, HD), BF),
        ((32, 16, HD), F32),
        ((16, 16, HD), F32),
        ((16, 16, HD), F32),
        ((16, 16, HD), F32),
        ((16, 16, HD), F32),
        ((16, 16, HD), F32),
        ((2, 16, D), BF),
        ((32, 16, HD), F32),
        ((2, 16, D), BF),
        ((7, 16, HD), F32),
    ]
    sems = [20, 20, 20, 20, 30, 30, 30, 30, 6, 6, 9, 4, 12, 12, 3, 3]
    outs = pl.pallas_call(
        kernel,
        out_shape=(
            jax.ShapeDtypeStruct((2, 16, D), BF),
            jax.ShapeDtypeStruct((1, D), BF),
            jax.ShapeDtypeStruct((2, 2, 16, D), BF),
            jax.ShapeDtypeStruct((2, 1, D), BF),
        ),
        in_specs=[hbm, vmem, hbm, smem, vmem, vmem, smem, hbm, hbm, hbm, hbm, vmem, vmem],
        out_specs=(vmem, vmem, vmem, vmem),
        scratch_shapes=[pltpu.VMEM(shape, dtype) for shape, dtype in scratch]
        + [pltpu.SemaphoreType.DMA((count,)) for count in sems],
        compiler_params=pltpu.CompilerParams(
            collective_id=0, has_side_effects=True, vmem_limit_bytes=60 * 1024 * 1024
        ),
        name="decoder_layer",
    )(
        prompt_states,
        decode_states,
        cache,
        prompt_starts,
        decode_lengths[None, :],
        decode_slots[None, :],
        decode_slots,
        jnp.swapaxes(w_qkv, 1, 2),
        w_out,
        w_gate_up,
        w_down,
        gains,
        jnp.asarray(freq),
    )
    return outs


def solution(mesh):
    in_specs = (
        P("dp", "tensor", None),
        P(("dp", "tensor"), None),
        P(None, "dp", "tensor", None),
        P(),
        P(),
        P(),
        P(None, None, "tensor"),
        P("tensor", None),
        P(None, None, "tensor"),
        P("tensor", None),
        P(),
    )
    out_specs = (
        P("dp", "tensor", None),
        P(("dp", "tensor"), None),
        P(None, "dp", "tensor", None),
        P(None, ("dp", "tensor"), None),
    )
    return jax.shard_map(local, mesh=mesh, in_specs=in_specs, out_specs=out_specs, check_vma=False)
```

```python
import jax
import jax.numpy as jnp
import numpy as np
from jax import lax
from jax.experimental import pallas as pl
from jax.experimental.pallas import tpu as pltpu
from jax.sharding import PartitionSpec as P

D = 2048
HD = 128
HEADS = 16
FFD = 256
CTX = 48
EPSILON = 1e-06
ROPE_BASE = 500000.0
MASKED_SCORE = -1e30
LOG2E = 1.4426950408889634
SCALE = HD ** (-0.5)
BF = jnp.bfloat16
F32 = jnp.float32
MESH = pl.DeviceIdType.MESH
NT = (((1,), (1,)), ((), ()))


def mul(value, factor):
    return pl.multiple_of(value * factor, factor)


def remote(src, dst, send_sem, recv_sem, dev):
    return pltpu.make_async_remote_copy(
        src_ref=src,
        dst_ref=dst,
        send_sem=send_sem,
        recv_sem=recv_sem,
        device_id={"tensor": dev},
        device_id_type=MESH,
    )


class Plane:
    def __init__(self):
        self.y = lax.axis_index("dp")
        self.t = lax.axis_index("tensor")
        self.c = lax.rem(self.t, 2)
        self.q = lax.div(self.t, 2)
        x = lax.rem(self.q, 4)
        z = lax.div(self.q, 4)
        self.a = x + self.c * (z - x)
        self.b = z + self.c * (x - z)
        self.sib = self.t + 1 - 2 * self.c
        self.aR, self.aO, self.aL = [lax.rem(self.a + i, 4) for i in (1, 2, 3)]
        self.bR, self.bO, self.bL = [lax.rem(self.b + i, 4) for i in (1, 2, 3)]

    def chip(self, a, b):
        return a * (1 + 3 * self.c) + b * (4 - 3 * self.c)

    def dev(self, a, b):
        return 2 * self.chip(a, b) + self.c


def block(buf, chip):
    return buf.at[pl.ds(mul(chip, 32), 32)]


def half(buf, chip, h):
    return buf.at[pl.ds(mul(chip * 2 + h, 16), 16)]


def gather_steps(p, buf, ss, rs, sends):
    def send(slot, ref, dev):
        copy = remote(ref, ref, ss.at[slot], rs.at[slot], dev)
        copy.start()
        sends.append(copy)

    def recv(slot, ref):
        remote(ref, ref, ss.at[slot], rs.at[slot], p.dev(p.aR, p.b)).wait_recv()

    def blk(a, b):
        return block(buf, p.chip(a, b))

    def hlf(a, b, h):
        return half(buf, p.chip(a, b), h)

    a, b, aR, aL, aO, bR, bL, bO = p.a, p.b, p.aR, p.aL, p.aO, p.bR, p.bL, p.bO
    to_aR, to_aL, to_bR, to_bL = p.dev(aR, b), p.dev(aL, b), p.dev(a, bR), p.dev(a, bL)
    own = blk(a, b)
    send(0, own, to_aR)
    send(1, own, to_aL)
    send(4, own, to_bR)
    send(5, own, to_bL)
    yield
    recv(0, blk(aL, b))
    send(2, hlf(aL, b, 0), to_aR)
    send(8, blk(aL, b), to_bR)
    send(9, blk(aL, b), to_bL)
    recv(1, blk(aR, b))
    send(3, hlf(aR, b, 1), to_aL)
    send(12, blk(aR, b), to_bR)
    send(13, blk(aR, b), to_bL)
    yield
    recv(4, blk(a, bL))
    send(6, hlf(a, bL, 0), to_bR)
    recv(5, blk(a, bR))
    send(7, hlf(a, bR, 1), to_bL)
    yield
    recv(2, hlf(aO, b, 0))
    recv(3, hlf(aO, b, 1))
    send(16, blk(aO, b), to_bR)
    send(17, blk(aO, b), to_bL)
    yield
    columns = (a, aL, aR, aO)
    for k in (1, 2, 3):
        recv(4 + 4 * k, blk(columns[k], bL))
        send(6 + 4 * k, hlf(columns[k], bL, 0), to_bR)
        recv(5 + 4 * k, blk(columns[k], bR))
        send(7 + 4 * k, hlf(columns[k], bR, 1), to_bL)
        yield
        for done in (k - 1,) if k < 3 else (2, 3):
            recv(6 + 4 * done, hlf(columns[done], bO, 0))
            recv(7 + 4 * done, hlf(columns[done], bO, 1))
            yield columns[done]


def reduce_steps(p, buf, land, ss, rs, sends, out, make=None):
    def send(slot, ref, dev):
        copy = remote(ref, land.at[slot], ss.at[slot], rs.at[slot], dev)
        copy.start()
        sends.append(copy)

    def recv(slot):
        remote(land.at[slot], land.at[slot], ss.at[slot], rs.at[slot], p.dev(p.aR, p.b)).wait_recv()
        return land[slot].astype(F32)

    def hlf(a, b, h):
        return half(buf, p.chip(a, b), h)

    def add(ref, slots):
        total = ref[...].astype(F32)
        for slot in slots:
            total = total + recv(slot)
        return total

    a, b, aR, aL, aO, bR, bL, bO = p.a, p.b, p.aR, p.aL, p.aO, p.bR, p.bL, p.bO
    to_aR, to_aL, to_bR, to_bL = p.dev(aR, b), p.dev(aL, b), p.dev(a, bR), p.dev(a, bL)
    columns = {0: a, 1: aL, 2: aR, 3: aO}

    def first_hop(k):
        send(6 * k + 0, hlf(columns[k], bO, 0), to_bL)
        send(6 * k + 1, hlf(columns[k], bO, 1), to_bR)

    def second_hop(k):
        send(6 * k + 2, hlf(columns[k], bL, 1), to_bL)
        send(6 * k + 3, hlf(columns[k], bR, 0), to_bR)
        ref = hlf(columns[k], bL, 0)
        ref[...] = add(ref, (6 * k + 0,)).astype(BF)
        send(6 * k + 4, ref, to_bL)
        ref = hlf(columns[k], bR, 1)
        ref[...] = add(ref, (6 * k + 1,)).astype(BF)
        send(6 * k + 5, ref, to_bR)

    def column_sum(k):
        h0, h1 = hlf(columns[k], b, 0), hlf(columns[k], b, 1)
        h0[...] = add(h0, (6 * k + 3, 6 * k + 4)).astype(BF)
        h1[...] = add(h1, (6 * k + 2, 6 * k + 5)).astype(BF)
        return h0, h1

    for k in (3, 1, 2, 0):
        if make is not None:
            make(columns[k])
        first_hop(k)
    second_hop(3)
    yield
    second_hop(1)
    yield
    h0, h1 = column_sum(3)
    send(24, h0, to_aL)
    send(25, h1, to_aR)
    second_hop(2)
    yield
    h0, h1 = column_sum(1)
    send(26, h1, to_aL)
    second_hop(0)
    yield
    h0[...] = add(h0, (24,)).astype(BF)
    send(28, h0, to_aL)
    h0, h1 = column_sum(2)
    send(27, h0, to_aR)
    h1[...] = add(h1, (25,)).astype(BF)
    send(29, h1, to_aR)
    yield
    h0, h1 = column_sum(0)
    yield
    out.append(jnp.concatenate([add(h0, (27, 28)), add(h1, (26, 29))], axis=0))


def run(steps, tasks):
    tasks = list(tasks)
    for step in steps:
        if tasks:
            tasks.pop(0)()
    for task in tasks:
        task()


def turn(values, cosine, sine):
    lane = lax.broadcasted_iota(jnp.int32, values.shape, 1)
    swapped = jnp.where(lane % 2 == 0, pltpu.roll(values, HD - 1, 1), pltpu.roll(values, 1, 1))
    return values * cosine + swapped * sine


def angles(positions, freq):
    turned = positions * freq
    lane = lax.broadcasted_iota(jnp.int32, turned.shape, 1)
    return jnp.cos(turned), jnp.where(lane % 2 == 0, -1.0, 1.0) * jnp.sin(turned)


def kernel(
    prompt_states,
    decode_states,
    cache,
    prompt_starts,
    lengths,
    slots_row,
    slots,
    w_qkv,
    w_out,
    w_gate_up,
    w_down,
    gains,
    freq,
    prompt_out,
    decode_out,
    new_prompt_kv,
    new_decode_kv,
    X1,
    X2,
    Y,
    Y2,
    RB1,
    RB2,
    WQ,
    WO,
    WG,
    WD,
    KD,
    VD,
    CK,
    QR,
    KN,
    NKV,
    ACT,
    SS,
    DX,
    XD,
    DQ,
    DKV,
    QH,
    KH,
    LEN,
    DCS,
    OBF,
    OB,
    SB,
    OR,
    SR,
    DY,
    DR,
    DX2,
    DY2,
    DR2,
    PO,
    FIN,
    FS,
    FD,
    WIDE,
    WIDE3,
    TURNED,
    g1s,
    g1r,
    g2s,
    g2r,
    r1s,
    r1r,
    r2s,
    r2r,
    ws,
    wr,
    wl,
    ls,
    ms,
    mr,
    ys,
    yr,
):
    p = Plane()
    y, t, c, q, sib = p.y, p.t, p.c, p.q, p.sib
    sends = []
    lanes_q = pl.ds(mul(q, HD), HD)
    own_block = pl.ds(mul(q, 32), 32)

    barrier = pltpu.get_barrier_semaphore()

    @pl.loop(1, 32)
    def _(i):
        pl.semaphore_signal(
            barrier, inc=1, device_id={"tensor": lax.rem(t + i, 32)}, device_id_type=MESH
        )

    for i in (1, 2, 3):
        pl.semaphore_signal(barrier, inc=1, device_id={"dp": lax.rem(y + i, 4)}, device_id_type=MESH)

    def plane_peers(body):
        @pl.loop(1, 16)
        def _(i):
            chip = lax.rem(q + i, 16)
            body(chip, 2 * chip + c)

    def group_peers(body, first=1, last=32):
        @pl.loop(first, last)
        def _(i):
            body(lax.rem(t + i, 32))

    def drain_recv(ref, sem):
        remote(ref, ref, sem, sem, sib).wait_recv()

    def drain_send(ref, sem):
        remote(ref, ref, sem, sem, sib).wait_send()

    def local_copy(src, dst, sem):
        copy = pltpu.make_async_copy(src, dst, sem)
        copy.start()
        return copy

    piece_here = local_copy(prompt_states.at[c], half(X1, q, c), wl.at[0])
    weight_pairs = (
        (w_qkv, WQ.at[:, c]),
        (w_out, WO.at[c]),
        (w_gate_up, WG.at[c]),
        (w_down, WD.at[c]),
    )
    weights_here = [local_copy(src, dst, wl.at[1 + i]) for i, (src, dst) in enumerate(weight_pairs)]

    def cache_slice(dev):
        return cache.at[:, lax.rem(dev, 2), :, pl.ds(mul(lax.div(dev, 2), HD), HD)]

    loads = [
        local_copy(
            cache.at[kv, pl.ds(2 + 16 * part, 16)], dst.at[pl.ds(16 * part, 16)], ls.at[2 * kv + part]
        )
        for part in range(2)
        for kv, dst in ((0, KD), (1, VD))
    ]
    own_cache = local_copy(cache_slice(t), CK.at[:, t], wl.at[5])

    for j in range(HEADS):
        WIDE[pl.ds(j, 1), :] = decode_states[:, j * HD : (j + 1) * HD].astype(F32)
    DX[q] = WIDE[0:16, :].astype(BF)

    slot_row = lax.broadcasted_iota(jnp.int32, (32, HD), 0)
    slot_id = 32 * y + 2 * (slot_row % 16) + slot_row // 16
    matched = jnp.where(slots_row[...] == slot_id, lengths[...].astype(F32), 0.0)
    LEN[...] = jnp.broadcast_to(jnp.sum(matched, axis=1, keepdims=True), (32, HD))
    cosine, sine = angles(LEN[...], freq[...])
    DCS[0] = cosine
    DCS[1] = sine

    pl.semaphore_wait(barrier, 34)

    piece = remote(prompt_states.at[1 - c], half(X1, q, c), ws.at[0], wr.at[0], sib)
    piece.start()
    plane_peers(lambda chip, dev: remote(DX.at[q], DX.at[q], ms.at[0], mr.at[0], dev).start())
    weights_there = []
    for i, (src, dst) in enumerate(weight_pairs):
        weights_there.append(remote(src, dst, ws.at[1 + i], wr.at[1 + i], sib))
        weights_there[i].start()

    def weight_here(i):
        weights_here[i].wait()
        weights_there[i].wait_recv()

    piece_here.wait()
    piece.wait_recv()
    steps = gather_steps(p, X1, g1s, g1r, sends)
    next(steps)

    def rows_of(landed):
        WIDE3[...] = landed[...].astype(F32)
        return jnp.concatenate([WIDE3[:, j, :] for j in range(HEADS)], axis=1).astype(BF)

    def project(rows):
        return lax.dot_general(rows, WQ[...].reshape(3 * HD, D), NT, preferred_element_type=F32)

    drain_recv(DX.at[pl.ds(0, 15)], mr.at[0])
    XD[...] = rows_of(DX)
    weight_here(0)
    dec = project(XD[...]).astype(BF)
    DQ[c, :, lanes_q] = dec[:, :HD]
    DKV[0, :, lanes_q] = dec[:, HD : 2 * HD]
    DKV[1, :, lanes_q] = dec[:, 2 * HD :]
    q_own = DQ.at[c, :, lanes_q]
    kv_own = DKV.at[:, :, lanes_q]
    group_peers(lambda dev: remote(q_own, q_own, ms.at[2], mr.at[2], dev).start())
    plane_peers(lambda chip, dev: remote(kv_own, kv_own, ms.at[3], mr.at[3], dev).start())
    next(steps)

    def send_cache(first, last):
        group_peers(
            lambda dev: remote(cache_slice(dev), CK.at[:, t], ms.at[1], mr.at[1], dev).start(),
            first,
            last,
        )

    next(steps)
    next(steps)

    drain_recv(OR.at[pl.ds(0, 31)], mr.at[2])
    drain_recv(KN.at[:, pl.ds(0, 240)], mr.at[3])

    def normed(raw, gain_row, first):
        scale = lax.rsqrt(jnp.mean(raw * raw, axis=1, keepdims=True) + EPSILON)
        rows = raw.shape[0]
        cos_part, sin_part = DCS[0, pl.ds(first, rows), :], DCS[1, pl.ds(first, rows), :]
        parts = []
        for j in range(HEADS):
            lanes = slice(j * HD, (j + 1) * HD)
            scaled = raw[:, lanes] * scale * gains[gain_row : gain_row + 1, lanes]
            parts.append(turn(scaled, cos_part, sin_part).astype(BF).astype(F32))
        return parts

    for plane in range(2):
        for j, part in enumerate(normed(DQ[plane].astype(F32), 0, 16 * plane)):
            QH[16 * plane : 16 * plane + 16, j * HD : (j + 1) * HD] = part
    for j, part in enumerate(normed(DKV[0].astype(F32), 1, mul(c, 16))):
        KH[:, j * HD : (j + 1) * HD] = part
    for load in loads:
        load.wait()

    own_lane = lax.broadcasted_iota(jnp.int32, (HEADS, D), 1) // HD
    own_row = lax.broadcasted_iota(jnp.int32, (HEADS, D), 0)
    own_head = own_lane == own_row
    spot = (lax.broadcasted_iota(jnp.int32, (HEADS, CTX), 1) + CTX * t).astype(F32)
    stat_lane = lax.broadcasted_iota(jnp.int32, (HEADS, HD), 1)

    done = 0

    def decode_slots_at(r):
        for plane in range(2):
            tops, totals = [], []
            for upper in range(2):
                row = 8 * upper + r
                index = 16 * plane + row
                slot = 2 * row + plane
                spread = jnp.where(own_head, QH[pl.ds(index, 1), :], 0.0).astype(BF)
                scores = lax.dot_general(spread, KD[slot], NT, preferred_element_type=F32)
                live = spot < LEN[pl.ds(index, 1), :CTX]
                scores = jnp.where(live, scores * SCALE, MASKED_SCORE)
                top = jnp.max(scores, axis=1, keepdims=True)
                probs = jnp.where(live, jnp.exp(scores - top), 0.0)
                tops.append(top)
                totals.append(jnp.sum(probs, axis=1, keepdims=True))
                mixed = jnp.dot(probs.astype(BF), VD[slot], preferred_element_type=F32)
                OBF[pl.ds(index, 1), :] = jnp.sum(
                    jnp.where(own_head, mixed, 0.0), axis=0, keepdims=True
                )
            SB[plane, :, r, :] = jnp.where(
                stat_lane < 64,
                jnp.where(stat_lane < 32, tops[0], totals[0]),
                jnp.where(stat_lane < 96, tops[1], totals[1]),
            )

    stat_row = lax.broadcasted_iota(jnp.int32, (8, HD), 0)
    SS[q] = jnp.zeros((8, HD), F32)

    def column_blocks(a):
        return [pl.ds(mul(p.chip(a, i), 32), 32) for i in range(4)]

    def row_sums(values):
        total = jnp.sum(values * values, axis=1, keepdims=True)
        return jnp.broadcast_to(total, (HD, HD)).T[0:8, :]

    def column_project(a):
        rows = pl.ds(mul(a, HD), HD)
        got = project(jnp.concatenate([X1[place, :] for place in column_blocks(a)], axis=0)).astype(BF)
        QR[rows, :] = got[:, :HD]
        KN[0, rows, :] = got[:, HD : 2 * HD]
        KN[1, rows, :] = got[:, 2 * HD :]
        query_sum = row_sums(got[:, :HD].astype(F32))
        key_sum = row_sums(got[:, HD : 2 * HD].astype(F32))
        SS[q] = jnp.where(
            stat_row == a, query_sum, jnp.where(stat_row == 4 + a, key_sum, SS[q])
        )

    turn_no = 0
    for step in steps:
        if step is None:
            if turn_no == 2:
                send_cache(1, 16)
            turn_no += 1
        else:
            column_project(step)
        if done < 8:
            decode_slots_at(done)
            done += 1
    plane_peers(lambda chip, dev: remote(SS.at[q], SS.at[q], ms.at[6], mr.at[6], dev).start())
    send_cache(16, 32)
    for r in range(done, 8):
        decode_slots_at(r)

    OB[0] = OBF[0:16, :].astype(BF)
    OB[1] = OBF[16:32, :].astype(BF)

    def mixed_slice(dev):
        return OB.at[lax.rem(dev, 2), :, pl.ds(mul(lax.div(dev, 2), HD), HD)]

    def stat_slice(dev):
        return SB.at[lax.rem(dev, 2), lax.div(dev, 2)]

    own_mixed = local_copy(mixed_slice(t), OR.at[t], wl.at[6])
    own_stat = local_copy(stat_slice(t), SR.at[t], wl.at[7])

    def send_partial(dev):
        remote(mixed_slice(dev), OR.at[t], ms.at[4], mr.at[4], dev).start()
        remote(stat_slice(dev), SR.at[t], ms.at[5], mr.at[5], dev).start()

    group_peers(send_partial)

    start = prompt_starts[2 * y + c]

    def offsets_of(index):
        chips = (index // HD) * (1 + 3 * c) + (index // 32 % 4) * (4 - 3 * c)
        return chips * 32 + index % 32

    for i in range(4):
        rows = slice(i * HD, (i + 1) * HD)
        offset = offsets_of(lax.broadcasted_iota(jnp.int32, (HD, HD), 0) + i * HD)
        cosine, sine = angles((offset + start).astype(F32), freq[...])
        for kind in range(2):
            raw = (QR[rows, :] if kind == 0 else KN[0, rows, :]).astype(F32)
            TURNED[kind, rows, :] = turn(raw * gains[kind : kind + 1, lanes_q], cosine, sine)
    drain_recv(SS.at[pl.ds(0, 15)], mr.at[6])
    scales = lax.rsqrt(jnp.sum(SS[...], axis=0) * (1.0 / D) + EPSILON)
    for i in range(4):
        rows = slice(i * HD, (i + 1) * HD)
        for kind in range(2):
            column = jnp.broadcast_to(scales[4 * kind + i : 4 * kind + i + 1, :], (HD, HD)).T
            turned = (TURNED[kind, rows, :] * column).astype(BF)
            if kind == 0:
                QR[rows, :] = turned
            else:
                KN[0, rows, :] = turned

    def fresh_slice(dev):
        chip = lax.div(dev, 2)
        low, high = lax.rem(chip, 4), lax.div(chip, 4)
        a, b = low + c * (high - low), high + c * (low - high)
        return KN.at[:, pl.ds(mul(8 * a + 2 * b + lax.rem(dev, 2), 16), 16), :]

    landing = NKV.at[:, c, :, lanes_q]
    own_fresh = local_copy(fresh_slice(t), landing, wl.at[8])
    group_peers(lambda dev: remote(fresh_slice(dev), landing, ms.at[7], mr.at[7], dev).start())

    own_mixed.wait()
    own_stat.wait()
    drain_recv(OR.at[pl.ds(0, 31)], mr.at[4])
    drain_recv(SR.at[pl.ds(0, 31)], mr.at[5])

    def stat(lane):
        parts = [
            jnp.broadcast_to(SR[:, :, lane + 64 * k : lane + 64 * k + 1], (32, 8, HD)) for k in (0, 1)
        ]
        return jnp.concatenate(parts, axis=1)

    tops, totals = stat(0), stat(32)
    own_rows = pl.ds(mul(c, 16), 16)
    own_score = (
        jnp.sum(QH[own_rows, lanes_q] * KH[:, lanes_q], axis=1, keepdims=True) * SCALE
    )
    highest = jnp.maximum(jnp.max(tops, axis=0), own_score)
    factors = jnp.exp(tops - highest[None])
    own_weight = jnp.exp(own_score - highest)
    total = jnp.sum(totals * factors, axis=0) + own_weight
    mixed = jnp.sum(OR[...].astype(F32) * factors, axis=0)
    mixed = mixed + own_weight.astype(BF).astype(F32) * DKV[1, :, lanes_q].astype(F32)
    attended_rows = (mixed / total).astype(BF)

    weight_here(1)

    def spread_decode(tail, staged, landed, index):
        for j in range(HEADS):
            WIDE3[:, j, :] = tail[:, j * HD : (j + 1) * HD]
        staged[...] = WIDE3[...].astype(BF)
        landed[q] = staged[q]
        plane_peers(
            lambda chip, dev: remote(
                staged.at[chip], landed.at[q], ms.at[index], mr.at[index], dev
            ).start()
        )

    def row_of(gain):
        parts = [gains[gain : gain + 1, j * HD : (j + 1) * HD] for j in range(HEADS)]
        return jnp.concatenate(parts, axis=0)

    def add_normed_rows(base, total, gain):
        scale = lax.rsqrt(jnp.mean(total * total, axis=1, keepdims=True) + EPSILON)
        return (base + total * scale * gains[gain : gain + 1, :]).astype(BF)

    def add_normed_row(base, landed, gain):
        total = jnp.sum(landed[...].astype(F32), axis=0)
        square = jnp.sum(total * total, axis=1, keepdims=True)
        mean = jnp.sum(square, axis=0, keepdims=True) * (1.0 / D)
        scale = lax.rsqrt(mean + EPSILON)
        return (base.astype(F32) + total * scale * row_of(gain)).astype(BF)

    w_head = WO[...].reshape(HD, D)
    spread_decode(jnp.dot(attended_rows, w_head, preferred_element_type=F32), DY, DR, 8)

    own_cache.wait()
    drain_recv(CK.at[:, pl.ds(0, 31)], mr.at[1])
    cached_spot = lax.broadcasted_iota(jnp.int32, (1, 32 * CTX), 1)
    cached_bias = jnp.where(cached_spot < start, 0.0, MASKED_SCORE)

    def column_attend(a):
        query = QR[pl.ds(mul(a, HD), HD), :]
        cached_keys = CK[0].reshape(32 * CTX, HD)
        cached_values = CK[1].reshape(32 * CTX, HD)
        fresh = lax.dot_general(query, KN[0], NT, preferred_element_type=F32)
        cached = lax.dot_general(query, cached_keys, NT, preferred_element_type=F32)
        column = offsets_of(lax.broadcasted_iota(jnp.int32, (1, 512), 1))
        row = offsets_of(lax.broadcasted_iota(jnp.int32, (HD, 1), 0) + a * HD)
        fresh = jnp.where(column <= row, fresh, MASKED_SCORE)
        cached = cached + cached_bias
        top = jnp.maximum(
            jnp.max(fresh, axis=1, keepdims=True), jnp.max(cached, axis=1, keepdims=True)
        )
        fresh = jnp.exp2((fresh - top) * (SCALE * LOG2E))
        cached = jnp.exp2((cached - top) * (SCALE * LOG2E))
        total = jnp.sum(fresh, axis=1, keepdims=True) + jnp.sum(cached, axis=1, keepdims=True)
        mixed = jnp.dot(fresh.astype(BF), KN[1], preferred_element_type=F32)
        mixed = mixed + jnp.dot(cached.astype(BF), cached_values, preferred_element_type=F32)
        result = jnp.dot(
            (mixed / total).astype(BF), w_head, preferred_element_type=F32
        ).astype(BF)
        for i, place in enumerate(column_blocks(a)):
            Y[place, :] = result[32 * i : 32 * i + 32]

    def hidden_row():
        drain_recv(DR.at[pl.ds(0, 15)], mr.at[8])
        DX2[q] = add_normed_row(DX[q], DR, 2)
        plane_peers(lambda chip, dev: remote(DX2.at[q], DX2.at[q], ms.at[9], mr.at[9], dev).start())

    attn_rows = []
    nothing = lambda: None
    run(
        reduce_steps(p, Y, RB1, r1s, r1r, sends, attn_rows, column_attend),
        [nothing, nothing, hidden_row],
    )
    X2[own_block, :] = add_normed_rows(X1[own_block, :].astype(F32), attn_rows[0], 2)
    steps = gather_steps(p, X2, g2s, g2r, sends)
    next(steps)

    weight_here(2)
    weight_here(3)

    def gated(hidden, core):
        gate = jnp.dot(hidden, WG[core, 0], preferred_element_type=F32)
        up = jnp.dot(hidden, WG[core, 1], preferred_element_type=F32)
        return (gate / (1.0 + jnp.exp(-gate)) * up).astype(BF)

    def down(pair):
        return jnp.dot(pair[0], WD[0], preferred_element_type=F32) + jnp.dot(
            pair[1], WD[1], preferred_element_type=F32
        )

    def decode_ffn():
        drain_recv(DX2.at[pl.ds(0, 15)], mr.at[9])
        hidden = rows_of(DX2)
        spread_decode(down([gated(hidden, core) for core in range(2)]), DY2, DR2, 10)

    def final_row():
        drain_recv(DR2.at[pl.ds(0, 15)], mr.at[10])
        FIN[t] = add_normed_row(DX2[q], DR2, 3)
        group_peers(lambda dev: remote(FIN.at[t], FIN.at[t], ms.at[11], mr.at[11], dev).start())

    def column_gated(a):
        hidden = jnp.concatenate([X2[rows, :] for rows in column_blocks(a)], axis=0)
        for core in range(2):
            ACT[core, pl.ds(mul(a, HD), HD), :] = gated(hidden, core)

    def column_down(a):
        rows = pl.ds(mul(a, HD), HD)
        result = down([ACT[0, rows, :], ACT[1, rows, :]]).astype(BF)
        for i, place in enumerate(column_blocks(a)):
            Y2[place, :] = result[32 * i : 32 * i + 32]

    mine = lax.broadcasted_iota(jnp.int32, (16, D), 0) == q

    def own_row_of(rows):
        return jnp.sum(jnp.where(mine, rows, 0.0), axis=0, keepdims=True).astype(BF)

    def fresh_out():
        own_fresh.wait()
        drain_recv(KN.at[:, pl.ds(0, 496)], mr.at[7])
        new_prompt_kv[...] = NKV[...]
        new_decode_kv[0, 0:1, :] = own_row_of(KH[...])
        new_decode_kv[0, 1:2, :] = own_row_of(DKV[1].astype(F32))

    tasks = [nothing, decode_ffn, fresh_out, final_row]
    for step in steps:
        if step is not None:
            column_gated(step)
        elif tasks:
            tasks.pop(0)()
    for task in tasks:
        task()

    slot_of = lax.broadcasted_iota(jnp.int32, (32, 16, HD), 0) + 32 * y
    crossing = []

    def wanted_row(yy):
        wanted = slots[32 * yy + t]
        return jnp.sum(jnp.where(slot_of == wanted, FIN[...].astype(F32), 0.0), axis=0)

    def cross_rows():
        drain_recv(FIN.at[pl.ds(0, 31)], mr.at[11])
        FD[0] = wanted_row(y)
        for i in (1, 2, 3):
            other = lax.rem(y + i, 4)
            FD[3 + i] = wanted_row(other)
            copy = pltpu.make_async_remote_copy(
                src_ref=FD.at[3 + i],
                dst_ref=FD.at[i],
                send_sem=ys.at[i - 1],
                recv_sem=yr.at[i - 1],
                device_id={"dp": other},
                device_id_type=MESH,
            )
            copy.start()
            crossing.append(copy)

    def decode_rows_out():
        result = FD[0]
        for i, copy in enumerate(crossing):
            copy.wait_recv()
            result = result + FD[1 + i]
        for j in range(HEADS):
            decode_out[:, j * HD : (j + 1) * HD] = result[j : j + 1, :].astype(BF)

    ffn_rows = []
    run(
        reduce_steps(p, Y2, RB2, r2s, r2r, sends, ffn_rows, column_down),
        [cross_rows, nothing, nothing, decode_rows_out],
    )
    out_rows = add_normed_rows(X2[own_block, :].astype(F32), ffn_rows[0], 3)
    FS[...] = out_rows.reshape(2, 16, D)
    swap = remote(FS.at[1 - c], PO.at[c], ws.at[5], wr.at[5], sib)
    swap.start()
    PO[c] = FS[c]

    for copy in sends + crossing + [piece]:
        copy.wait_send()
    for there in weights_there:
        there.wait_send()
    drain_send(DX.at[pl.ds(0, 15)], ms.at[0])
    drain_send(CK.at[:, pl.ds(0, 31)], ms.at[1])
    drain_send(OR.at[pl.ds(0, 31)], ms.at[2])
    drain_send(KN.at[:, pl.ds(0, 240)], ms.at[3])
    drain_send(OR.at[pl.ds(0, 31)], ms.at[4])
    drain_send(SR.at[pl.ds(0, 31)], ms.at[5])
    drain_send(SS.at[pl.ds(0, 15)], ms.at[6])
    drain_send(KN.at[:, pl.ds(0, 496)], ms.at[7])
    drain_send(DR.at[pl.ds(0, 15)], ms.at[8])
    drain_send(DX2.at[pl.ds(0, 15)], ms.at[9])
    drain_send(DR2.at[pl.ds(0, 15)], ms.at[10])
    drain_send(FIN.at[pl.ds(0, 31)], ms.at[11])
    swap.wait()
    prompt_out[...] = PO[...]


def place(*refs):
    for src, dst in zip(refs[:4], refs[4:]):
        dst[...] = src[...]


def local(
    prompt_states,
    decode_states,
    cache,
    prompt_starts,
    decode_lengths,
    decode_slots,
    w_qkv,
    w_out,
    w_gate_up,
    w_down,
    gains,
):
    freq = np.power(ROPE_BASE, -2.0 * (np.arange(HD) // 2) / HD).astype(np.float32)[None, :]
    vmem = pl.BlockSpec(memory_space=pltpu.VMEM)
    smem = pl.BlockSpec(memory_space=pltpu.SMEM)
    hbm = pl.BlockSpec(memory_space=pl.ANY)
    scratch = [
        ((512, D), BF),
        ((512, D), BF),
        ((512, D), BF),
        ((512, D), BF),
        ((30, 16, D), BF),
        ((30, 16, D), BF),
        ((3, 2, 64, D), BF),
        ((2, 64, D), BF),
        ((2, 2, D, FFD), BF),
        ((2, FFD, D), BF),
        ((32, CTX, D), BF),
        ((32, CTX, D), BF),
        ((2, 32, CTX, HD), BF),
        ((512, HD), BF),
        ((2, 512, HD), BF),
        ((2, 2, 16, D), BF),
        ((2, 512, FFD), BF),
        ((16, 8, HD), F32),
        ((16, 16, HD), BF),
        ((16, D), BF),
        ((2, 16, D), BF),
        ((2, 16, D), BF),
        ((32, D), F32),
        ((16, D), F32),
        ((32, HD), F32),
        ((2, 32, HD), F32),
        ((32, D), F32),
        ((2, 16, D), BF),
        ((2, 16, 8, HD), F32),
        ((32, 16, HD), BF),
        ((32, 8, HD), F32),
        ((16, 16, HD), BF),
        ((16, 16, HD), BF),
        ((16, 16, HD), BF),
        ((16, 16, HD), BF),
        ((16, 16, HD), BF),
        ((2, 16, D), BF),
        ((32, 16, HD), BF),
        ((2, 16, D), BF),
        ((7, 16, HD), F32),
        ((16, HD), F32),
        ((16, 16, HD), F32),
        ((2, 512, HD), F32),
    ]
    sems = [20, 20, 20, 20, 30, 30, 30, 30, 6, 6, 9, 4, 12, 12, 3, 3]
    outs = pl.pallas_call(
        kernel,
        out_shape=(
            jax.ShapeDtypeStruct((2, 16, D), BF),
            jax.ShapeDtypeStruct((1, D), BF),
            jax.ShapeDtypeStruct((2, 2, 16, D), BF),
            jax.ShapeDtypeStruct((1, 2, D), BF),
        ),
        in_specs=[hbm, vmem, hbm, smem, vmem, vmem, smem, hbm, hbm, hbm, hbm, vmem, vmem],
        out_specs=(vmem, vmem, vmem, vmem),
        scratch_shapes=[pltpu.VMEM(shape, dtype) for shape, dtype in scratch]
        + [pltpu.SemaphoreType.DMA((count,)) for count in sems],
        compiler_params=pltpu.CompilerParams(
            collective_id=0, has_side_effects=True, vmem_limit_bytes=60 * 1024 * 1024
        ),
        name="decoder_layer",
    )(
        prompt_states,
        decode_states,
        cache,
        prompt_starts,
        decode_lengths[None, :],
        decode_slots[None, :],
        decode_slots,
        jnp.swapaxes(w_qkv, 1, 2),
        w_out,
        w_gate_up,
        w_down,
        gains,
        jnp.asarray(freq),
    )
    placed = pl.pallas_call(
        place,
        out_shape=tuple(jax.ShapeDtypeStruct(out.shape, out.dtype) for out in outs),
        in_specs=[vmem] * 4,
        out_specs=(vmem,) * 4,
        name="place",
    )(*outs)
    return placed[0], placed[1], placed[2], jnp.swapaxes(placed[3], 0, 1)


def solution(mesh):
    in_specs = (
        P("dp", "tensor", None),
        P(("dp", "tensor"), None),
        P(None, "dp", "tensor", None),
        P(),
        P(),
        P(),
        P(None, None, "tensor"),
        P("tensor", None),
        P(None, None, "tensor"),
        P("tensor", None),
        P(),
    )
    out_specs = (
        P("dp", "tensor", None),
        P(("dp", "tensor"), None),
        P(None, "dp", "tensor", None),
        P(None, ("dp", "tensor"), None),
    )
    return jax.shard_map(local, mesh=mesh, in_specs=in_specs, out_specs=out_specs, check_vma=False)
```

```python
import jax
import jax.numpy as jnp
import numpy as np
from jax import lax
from jax.experimental import pallas as pl
from jax.experimental.pallas import tpu as pltpu
from jax.sharding import PartitionSpec as P

D = 2048
HD = 128
HEADS = 16
FFD = 256
CTX = 48
EPSILON = 1e-06
ROPE_BASE = 500000.0
MASKED_SCORE = -1e30
LOG2E = 1.4426950408889634
SCALE = HD ** (-0.5)
BF = jnp.bfloat16
F32 = jnp.float32
MESH = pl.DeviceIdType.MESH
NT = (((1,), (1,)), ((), ()))


def mul(value, factor):
    return pl.multiple_of(value * factor, factor)


def remote(src, dst, send_sem, recv_sem, dev):
    return pltpu.make_async_remote_copy(
        src_ref=src,
        dst_ref=dst,
        send_sem=send_sem,
        recv_sem=recv_sem,
        device_id={"tensor": dev},
        device_id_type=MESH,
    )


class Plane:
    def __init__(self):
        self.y = lax.axis_index("dp")
        self.t = lax.axis_index("tensor")
        self.c = lax.rem(self.t, 2)
        self.q = lax.div(self.t, 2)
        x = lax.rem(self.q, 4)
        z = lax.div(self.q, 4)
        self.a = x + self.c * (z - x)
        self.b = z + self.c * (x - z)
        self.sib = self.t + 1 - 2 * self.c
        self.aR, self.aO, self.aL = [lax.rem(self.a + i, 4) for i in (1, 2, 3)]
        self.bR, self.bO, self.bL = [lax.rem(self.b + i, 4) for i in (1, 2, 3)]

    def chip(self, a, b):
        return a * (1 + 3 * self.c) + b * (4 - 3 * self.c)

    def dev(self, a, b):
        return 2 * self.chip(a, b) + self.c


def block(buf, chip):
    return buf.at[pl.ds(mul(chip, 32), 32)]


def half(buf, chip, h):
    return buf.at[pl.ds(mul(chip * 2 + h, 16), 16)]


def gather_steps(p, buf, ss, rs, sends):
    def send(slot, ref, dev):
        copy = remote(ref, ref, ss.at[slot], rs.at[slot], dev)
        copy.start()
        sends.append(copy)

    def recv(slot, ref):
        remote(ref, ref, ss.at[slot], rs.at[slot], p.dev(p.aR, p.b)).wait_recv()

    def blk(a, b):
        return block(buf, p.chip(a, b))

    def hlf(a, b, h):
        return half(buf, p.chip(a, b), h)

    a, b, aR, aL, aO, bR, bL, bO = p.a, p.b, p.aR, p.aL, p.aO, p.bR, p.bL, p.bO
    to_aR, to_aL, to_bR, to_bL = p.dev(aR, b), p.dev(aL, b), p.dev(a, bR), p.dev(a, bL)
    own = blk(a, b)
    send(0, own, to_aR)
    send(1, own, to_aL)
    send(2, own, p.dev(aO, b))
    send(4, own, to_bR)
    send(5, own, to_bL)
    yield
    recv(0, blk(aL, b))
    send(8, blk(aL, b), to_bR)
    send(9, blk(aL, b), to_bL)
    recv(1, blk(aR, b))
    send(12, blk(aR, b), to_bR)
    send(13, blk(aR, b), to_bL)
    yield
    recv(4, blk(a, bL))
    send(6, hlf(a, bL, 0), to_bR)
    recv(5, blk(a, bR))
    send(7, hlf(a, bR, 1), to_bL)
    yield
    recv(2, blk(aO, b))
    send(16, blk(aO, b), to_bR)
    send(17, blk(aO, b), to_bL)
    yield
    columns = (a, aL, aR, aO)
    for k in (1, 2, 3):
        recv(4 + 4 * k, blk(columns[k], bL))
        send(6 + 4 * k, hlf(columns[k], bL, 0), to_bR)
        recv(5 + 4 * k, blk(columns[k], bR))
        send(7 + 4 * k, hlf(columns[k], bR, 1), to_bL)
        yield
        for done in ((), (), (0,), (1, 2, 3))[k]:
            recv(6 + 4 * done, hlf(columns[done], bO, 0))
            recv(7 + 4 * done, hlf(columns[done], bO, 1))
            yield columns[done]


class Reduce:
    def __init__(self, p, buf, land, ss, rs, sends):
        self.p, self.buf, self.land, self.ss, self.rs, self.sends = p, buf, land, ss, rs, sends
        self.columns = (p.a, p.aL, p.aR, p.aO)
        self.owners = [p.dev(column, p.b) for column in self.columns]
        self.to_bR, self.to_bL = p.dev(p.a, p.bR), p.dev(p.a, p.bL)

    def place(self, slot):
        return self.land.at[pl.ds(16 * slot, 16 if slot < 24 else 32)]

    def send(self, slot, ref, dev):
        copy = remote(ref, self.place(slot), self.ss.at[slot], self.rs.at[slot], dev)
        copy.start()
        self.sends.append(copy)

    def add(self, ref, slots):
        total = ref[...].astype(F32)
        for slot in slots:
            place = self.place(slot)
            remote(place, place, self.ss.at[slot], self.rs.at[slot], self.to_bR).wait_recv()
            total = total + place[...].astype(F32)
        return total

    def half(self, k, b, h):
        return half(self.buf, self.p.chip(self.columns[k], b), h)

    def first_hop(self, k):
        self.send(6 * k + 0, self.half(k, self.p.bO, 0), self.to_bL)
        self.send(6 * k + 1, self.half(k, self.p.bO, 1), self.to_bR)

    def leaves(self, k):
        self.send(6 * k + 2, self.half(k, self.p.bL, 1), self.to_bL)
        self.send(6 * k + 3, self.half(k, self.p.bR, 0), self.to_bR)

    def second_hop(self, k):
        ref = self.half(k, self.p.bL, 0)
        ref[...] = self.add(ref, (6 * k + 0,)).astype(BF)
        self.send(6 * k + 4, ref, self.to_bL)
        ref = self.half(k, self.p.bR, 1)
        ref[...] = self.add(ref, (6 * k + 1,)).astype(BF)
        self.send(6 * k + 5, ref, self.to_bR)

    def column_sum(self, k):
        h0, h1 = self.half(k, self.p.b, 0), self.half(k, self.p.b, 1)
        h0[...] = self.add(h0, (6 * k + 3, 6 * k + 4)).astype(BF)
        h1[...] = self.add(h1, (6 * k + 2, 6 * k + 5)).astype(BF)
        if k > 0:
            self.send(22 + 2 * k, block(self.buf, self.p.chip(self.columns[k], self.p.b)), self.owners[k])

    def own_sum(self):
        return self.add(block(self.buf, self.p.chip(self.p.a, self.p.b)), (24, 26, 28))


def turn(values, cosine, sine):
    lane = lax.broadcasted_iota(jnp.int32, values.shape, 1)
    swapped = jnp.where(lane % 2 == 0, pltpu.roll(values, HD - 1, 1), pltpu.roll(values, 1, 1))
    return values * cosine + swapped * sine


def angles(positions, freq):
    turned = positions * freq
    lane = lax.broadcasted_iota(jnp.int32, turned.shape, 1)
    return jnp.cos(turned), jnp.where(lane % 2 == 0, -1.0, 1.0) * jnp.sin(turned)


def kernel(
    prompt_states,
    decode_states,
    cache,
    prompt_starts,
    lengths,
    slots_row,
    slots,
    w_qkv,
    w_out,
    w_gate_up,
    w_down,
    gains,
    freq,
    prompt_out,
    decode_out,
    new_prompt_kv,
    new_decode_kv,
    X1,
    X2,
    Y,
    Y2,
    RB1,
    RB2,
    WQ,
    WO,
    WG,
    WD,
    KD,
    VD,
    CK,
    QR,
    KN,
    NKV,
    ACT,
    SS,
    DX,
    XD,
    DQ,
    DKV,
    QH,
    KH,
    LEN,
    DCS,
    OBF,
    OB,
    SB,
    OR,
    SR,
    DY,
    DR,
    DX2,
    DY2,
    DR2,
    PO,
    FIN,
    FS,
    FD,
    WIDE,
    WIDE3,
    TURNED,
    g1s,
    g1r,
    g2s,
    g2r,
    r1s,
    r1r,
    r2s,
    r2r,
    ws,
    wr,
    wl,
    ls,
    ms,
    mr,
    ys,
    yr,
):
    p = Plane()
    y, t, c, q, sib = p.y, p.t, p.c, p.q, p.sib
    sends = []
    lanes_q = pl.ds(mul(q, HD), HD)
    own_block = pl.ds(mul(q, 32), 32)

    barrier = pltpu.get_barrier_semaphore()

    @pl.loop(1, 32)
    def _(i):
        pl.semaphore_signal(
            barrier, inc=1, device_id={"tensor": lax.rem(t + i, 32)}, device_id_type=MESH
        )

    for i in (1, 2, 3):
        pl.semaphore_signal(barrier, inc=1, device_id={"dp": lax.rem(y + i, 4)}, device_id_type=MESH)

    def plane_peers(body):
        @pl.loop(1, 16)
        def _(i):
            chip = lax.rem(q + i, 16)
            body(chip, 2 * chip + c)

    def group_peers(body, first=1, last=32):
        @pl.loop(first, last)
        def _(i):
            body(lax.rem(t + i, 32))

    def drain_recv(ref, sem):
        remote(ref, ref, sem, sem, sib).wait_recv()

    def drain_send(ref, sem):
        remote(ref, ref, sem, sem, sib).wait_send()

    def local_copy(src, dst, sem):
        copy = pltpu.make_async_copy(src, dst, sem)
        copy.start()
        return copy

    piece_here = local_copy(prompt_states.at[c], half(X1, q, c), wl.at[0])
    weight_pairs = (
        (w_qkv, WQ.at[:, c]),
        (w_out, WO.at[c]),
        (w_gate_up, WG.at[c]),
        (w_down, WD.at[c]),
    )
    weights_here = [local_copy(src, dst, wl.at[1 + i]) for i, (src, dst) in enumerate(weight_pairs)]

    def cache_slice(dev):
        return cache.at[:, lax.rem(dev, 2), :, pl.ds(mul(lax.div(dev, 2), HD), HD)]

    own_cache = local_copy(cache_slice(t), CK.at[:, t], wl.at[5])

    for j in range(HEADS):
        WIDE[pl.ds(j, 1), :] = decode_states[:, j * HD : (j + 1) * HD].astype(F32)
    DX[q] = WIDE[0:16, :].astype(BF)

    slot_row = lax.broadcasted_iota(jnp.int32, (32, HD), 0)
    slot_id = 32 * y + 2 * (slot_row % 16) + slot_row // 16
    matched = jnp.where(slots_row[...] == slot_id, lengths[...].astype(F32), 0.0)
    LEN[...] = jnp.broadcast_to(jnp.sum(matched, axis=1, keepdims=True), (32, HD))
    cosine, sine = angles(LEN[...], freq[...])
    DCS[0] = cosine
    DCS[1] = sine

    pl.semaphore_wait(barrier, 34)

    piece = remote(prompt_states.at[1 - c], half(X1, q, c), ws.at[0], wr.at[0], sib)
    piece.start()
    plane_peers(lambda chip, dev: remote(DX.at[q], DX.at[q], ms.at[0], mr.at[0], dev).start())
    weights_there = []
    for i, (src, dst) in enumerate(weight_pairs):
        weights_there.append(remote(src, dst, ws.at[1 + i], wr.at[1 + i], sib))
    weights_there[0].start()
    loads = [
        local_copy(
            cache.at[kv, pl.ds(2 + 16 * part, 16)], dst.at[pl.ds(16 * part, 16)], ls.at[2 * kv + part]
        )
        for part in range(2)
        for kv, dst in ((0, KD), (1, VD))
    ]
    for i in (1, 2, 3):
        weights_there[i].start()

    def weight_here(i):
        weights_here[i].wait()
        weights_there[i].wait_recv()

    def send_cache(first, last):
        group_peers(
            lambda dev: remote(cache_slice(dev), CK.at[:, t], ms.at[1], mr.at[1], dev).start(),
            first,
            last,
        )

    send_cache(1, 8)
    piece_here.wait()
    piece.wait_recv()
    steps = gather_steps(p, X1, g1s, g1r, sends)
    next(steps)

    def rows_of(landed):
        WIDE3[...] = landed[...].astype(F32)
        return jnp.concatenate([WIDE3[:, j, :] for j in range(HEADS)], axis=1).astype(BF)

    def project(rows):
        return lax.dot_general(rows, WQ[...].reshape(3 * HD, D), NT, preferred_element_type=F32)

    next(steps)
    next(steps)
    drain_recv(DX.at[pl.ds(0, 15)], mr.at[0])
    XD[...] = rows_of(DX)
    weight_here(0)
    dec = project(XD[...]).astype(BF)
    DQ[c, :, lanes_q] = dec[:, :HD]
    DKV[0, :, lanes_q] = dec[:, HD : 2 * HD]
    DKV[1, :, lanes_q] = dec[:, 2 * HD :]
    q_own = DQ.at[c, :, lanes_q]
    kv_own = DKV.at[:, :, lanes_q]
    group_peers(lambda dev: remote(q_own, q_own, ms.at[2], mr.at[2], dev).start())
    plane_peers(lambda chip, dev: remote(kv_own, kv_own, ms.at[3], mr.at[3], dev).start())
    next(steps)

    def normed(raw, gain_row, first):
        scale = lax.rsqrt(jnp.mean(raw * raw, axis=1, keepdims=True) + EPSILON)
        rows = raw.shape[0]
        cos_part, sin_part = DCS[0, pl.ds(first, rows), :], DCS[1, pl.ds(first, rows), :]
        parts = []
        for j in range(HEADS):
            lanes = slice(j * HD, (j + 1) * HD)
            scaled = raw[:, lanes] * scale * gains[gain_row : gain_row + 1, lanes]
            parts.append(turn(scaled, cos_part, sin_part).astype(BF).astype(F32))
        return parts

    def decode_norms():
        drain_recv(OR.at[pl.ds(0, 31)], mr.at[2])
        drain_recv(KN.at[:, pl.ds(0, 240)], mr.at[3])
        for plane in range(2):
            for j, part in enumerate(normed(DQ[plane].astype(F32), 0, 16 * plane)):
                QH[16 * plane : 16 * plane + 16, j * HD : (j + 1) * HD] = part
        for j, part in enumerate(normed(DKV[0].astype(F32), 1, mul(c, 16))):
            KH[:, j * HD : (j + 1) * HD] = part
        for load in loads:
            load.wait()

    own_lane = lax.broadcasted_iota(jnp.int32, (HEADS, D), 1) // HD
    own_row = lax.broadcasted_iota(jnp.int32, (HEADS, D), 0)
    own_head = own_lane == own_row
    spot = (lax.broadcasted_iota(jnp.int32, (HEADS, CTX), 1) + CTX * t).astype(F32)
    stat_lane = lax.broadcasted_iota(jnp.int32, (HEADS, HD), 1)

    def decode_slots_at(r):
        for plane in range(2):
            tops, totals = [], []
            for upper in range(2):
                row = 8 * upper + r
                index = 16 * plane + row
                slot = 2 * row + plane
                spread = jnp.where(own_head, QH[pl.ds(index, 1), :], 0.0).astype(BF)
                scores = lax.dot_general(spread, KD[slot], NT, preferred_element_type=F32)
                live = spot < LEN[pl.ds(index, 1), :CTX]
                scores = jnp.where(live, scores * SCALE, MASKED_SCORE)
                top = jnp.max(scores, axis=1, keepdims=True)
                probs = jnp.where(live, jnp.exp(scores - top), 0.0)
                tops.append(top)
                totals.append(jnp.sum(probs, axis=1, keepdims=True))
                mixed = jnp.dot(probs.astype(BF), VD[slot], preferred_element_type=F32)
                OBF[pl.ds(index, 1), :] = jnp.sum(
                    jnp.where(own_head, mixed, 0.0), axis=0, keepdims=True
                )
            SB[plane, :, r, :] = jnp.where(
                stat_lane < 64,
                jnp.where(stat_lane < 32, tops[0], totals[0]),
                jnp.where(stat_lane < 96, tops[1], totals[1]),
            )

    stat_row = lax.broadcasted_iota(jnp.int32, (8, HD), 0)
    SS[q] = jnp.zeros((8, HD), F32)

    def column_blocks(a):
        return [pl.ds(mul(p.chip(a, i), 32), 32) for i in range(4)]

    def row_sums(values):
        total = jnp.sum(values * values, axis=1, keepdims=True)
        return jnp.broadcast_to(total, (HD, HD)).T[0:8, :]

    def column_project(a):
        rows = pl.ds(mul(a, HD), HD)
        got = project(jnp.concatenate([X1[place, :] for place in column_blocks(a)], axis=0)).astype(BF)
        QR[rows, :] = got[:, :HD]
        KN[0, rows, :] = got[:, HD : 2 * HD]
        KN[1, rows, :] = got[:, 2 * HD :]
        query_sum = row_sums(got[:, :HD].astype(F32))
        key_sum = row_sums(got[:, HD : 2 * HD].astype(F32))
        SS[q] = jnp.where(
            stat_row == a, query_sum, jnp.where(stat_row == 4 + a, key_sum, SS[q])
        )

    next(steps)
    next(steps)
    send_cache(8, 20)
    column_project(next(steps))
    decode_norms()
    next(steps)
    for r, column in enumerate(steps):
        column_project(column)
        if r < 2:
            decode_slots_at(r)
    plane_peers(lambda chip, dev: remote(SS.at[q], SS.at[q], ms.at[6], mr.at[6], dev).start())
    send_cache(20, 32)
    for r in range(2, 8):
        decode_slots_at(r)

    OB[0] = OBF[0:16, :].astype(BF)
    OB[1] = OBF[16:32, :].astype(BF)

    def mixed_slice(dev):
        return OB.at[lax.rem(dev, 2), :, pl.ds(mul(lax.div(dev, 2), HD), HD)]

    def stat_slice(dev):
        return SB.at[lax.rem(dev, 2), lax.div(dev, 2)]

    own_mixed = local_copy(mixed_slice(t), OR.at[t], wl.at[6])
    own_stat = local_copy(stat_slice(t), SR.at[t], wl.at[7])

    def send_partial(dev):
        remote(mixed_slice(dev), OR.at[t], ms.at[4], mr.at[4], dev).start()
        remote(stat_slice(dev), SR.at[t], ms.at[5], mr.at[5], dev).start()

    group_peers(send_partial)

    start = prompt_starts[2 * y + c]

    def offsets_of(index):
        chips = (index // HD) * (1 + 3 * c) + (index // 32 % 4) * (4 - 3 * c)
        return chips * 32 + index % 32

    for i in range(4):
        rows = slice(i * HD, (i + 1) * HD)
        offset = offsets_of(lax.broadcasted_iota(jnp.int32, (HD, HD), 0) + i * HD)
        cosine, sine = angles((offset + start).astype(F32), freq[...])
        for kind in range(2):
            raw = (QR[rows, :] if kind == 0 else KN[0, rows, :]).astype(F32)
            TURNED[kind, rows, :] = turn(raw * gains[kind : kind + 1, lanes_q], cosine, sine)
    drain_recv(SS.at[pl.ds(0, 15)], mr.at[6])
    scales = lax.rsqrt(jnp.sum(SS[...], axis=0) * (1.0 / D) + EPSILON)
    for i in range(4):
        rows = slice(i * HD, (i + 1) * HD)
        for kind in range(2):
            column = jnp.broadcast_to(scales[4 * kind + i : 4 * kind + i + 1, :], (HD, HD)).T
            turned = (TURNED[kind, rows, :] * column).astype(BF)
            if kind == 0:
                QR[rows, :] = turned
            else:
                KN[0, rows, :] = turned

    def fresh_slice(dev):
        chip = lax.div(dev, 2)
        low, high = lax.rem(chip, 4), lax.div(chip, 4)
        a, b = low + c * (high - low), high + c * (low - high)
        return KN.at[:, pl.ds(mul(8 * a + 2 * b + lax.rem(dev, 2), 16), 16), :]

    landing = NKV.at[:, c, :, lanes_q]
    own_fresh = local_copy(fresh_slice(t), landing, wl.at[8])
    group_peers(lambda dev: remote(fresh_slice(dev), landing, ms.at[7], mr.at[7], dev).start())

    own_mixed.wait()
    own_stat.wait()
    drain_recv(OR.at[pl.ds(0, 31)], mr.at[4])
    drain_recv(SR.at[pl.ds(0, 31)], mr.at[5])

    def stat(lane):
        parts = [
            jnp.broadcast_to(SR[:, :, lane + 64 * k : lane + 64 * k + 1], (32, 8, HD)) for k in (0, 1)
        ]
        return jnp.concatenate(parts, axis=1)

    tops, totals = stat(0), stat(32)
    own_rows = pl.ds(mul(c, 16), 16)
    own_score = (
        jnp.sum(QH[own_rows, lanes_q] * KH[:, lanes_q], axis=1, keepdims=True) * SCALE
    )
    highest = jnp.maximum(jnp.max(tops, axis=0), own_score)
    factors = jnp.exp(tops - highest[None])
    own_weight = jnp.exp(own_score - highest)
    total = jnp.sum(totals * factors, axis=0) + own_weight
    mixed = jnp.sum(OR[...].astype(F32) * factors, axis=0)
    mixed = mixed + own_weight.astype(BF).astype(F32) * DKV[1, :, lanes_q].astype(F32)
    attended_rows = (mixed / total).astype(BF)

    weight_here(1)

    def spread_decode(tail, staged, landed, index):
        for j in range(HEADS):
            WIDE3[:, j, :] = tail[:, j * HD : (j + 1) * HD]
        staged[...] = WIDE3[...].astype(BF)
        landed[q] = staged[q]
        plane_peers(
            lambda chip, dev: remote(
                staged.at[chip], landed.at[q], ms.at[index], mr.at[index], dev
            ).start()
        )

    def row_of(gain):
        parts = [gains[gain : gain + 1, j * HD : (j + 1) * HD] for j in range(HEADS)]
        return jnp.concatenate(parts, axis=0)

    def add_normed_rows(base, total, gain):
        scale = lax.rsqrt(jnp.mean(total * total, axis=1, keepdims=True) + EPSILON)
        return (base + total * scale * gains[gain : gain + 1, :]).astype(BF)

    def add_normed_row(base, landed, gain):
        total = jnp.sum(landed[...].astype(F32), axis=0)
        square = jnp.sum(total * total, axis=1, keepdims=True)
        mean = jnp.sum(square, axis=0, keepdims=True) * (1.0 / D)
        scale = lax.rsqrt(mean + EPSILON)
        return (base.astype(F32) + total * scale * row_of(gain)).astype(BF)

    w_head = WO[...].reshape(HD, D)
    spread_decode(jnp.dot(attended_rows, w_head, preferred_element_type=F32), DY, DR, 8)

    own_cache.wait()
    drain_recv(CK.at[:, pl.ds(0, 31)], mr.at[1])
    cached_spot = lax.broadcasted_iota(jnp.int32, (1, 32 * CTX), 1)
    cached_bias = jnp.where(cached_spot < start, 0.0, MASKED_SCORE)

    def column_attend(a):
        query = QR[pl.ds(mul(a, HD), HD), :]
        cached_keys = CK[0].reshape(32 * CTX, HD)
        cached_values = CK[1].reshape(32 * CTX, HD)
        fresh = lax.dot_general(query, KN[0], NT, preferred_element_type=F32)
        cached = lax.dot_general(query, cached_keys, NT, preferred_element_type=F32)
        column = offsets_of(lax.broadcasted_iota(jnp.int32, (1, 512), 1))
        row = offsets_of(lax.broadcasted_iota(jnp.int32, (HD, 1), 0) + a * HD)
        fresh = jnp.where(column <= row, fresh, MASKED_SCORE)
        cached = cached + cached_bias
        top = jnp.maximum(
            jnp.max(fresh, axis=1, keepdims=True), jnp.max(cached, axis=1, keepdims=True)
        )
        fresh = jnp.exp2((fresh - top) * (SCALE * LOG2E))
        cached = jnp.exp2((cached - top) * (SCALE * LOG2E))
        total = jnp.sum(fresh, axis=1, keepdims=True) + jnp.sum(cached, axis=1, keepdims=True)
        mixed = jnp.dot(fresh.astype(BF), KN[1], preferred_element_type=F32)
        mixed = mixed + jnp.dot(cached.astype(BF), cached_values, preferred_element_type=F32)
        result = jnp.dot(
            (mixed / total).astype(BF), w_head, preferred_element_type=F32
        ).astype(BF)
        for i, place in enumerate(column_blocks(a)):
            Y[place, :] = result[32 * i : 32 * i + 32]

    def hidden_row():
        drain_recv(DR.at[pl.ds(0, 15)], mr.at[8])
        DX2[q] = add_normed_row(DX[q], DR, 2)
        plane_peers(lambda chip, dev: remote(DX2.at[q], DX2.at[q], ms.at[9], mr.at[9], dev).start())

    first_sum = Reduce(p, Y, RB1, r1s, r1r, sends)
    for k in (3, 1, 2, 0):
        column_attend(first_sum.columns[k])
        first_sum.first_hop(k)
        first_sum.leaves(k)
        if k == 2:
            first_sum.second_hop(3)
    first_sum.second_hop(1)
    first_sum.column_sum(3)
    first_sum.second_hop(2)
    first_sum.column_sum(1)
    first_sum.second_hop(0)
    first_sum.column_sum(2)
    first_sum.column_sum(0)
    hidden_row()
    X2[own_block, :] = add_normed_rows(
        X1[own_block, :].astype(F32), first_sum.own_sum(), 2
    )
    steps = gather_steps(p, X2, g2s, g2r, sends)
    next(steps)

    weight_here(2)
    weight_here(3)

    def gated(hidden, core):
        gate = jnp.dot(hidden, WG[core, 0], preferred_element_type=F32)
        up = jnp.dot(hidden, WG[core, 1], preferred_element_type=F32)
        return (gate / (1.0 + jnp.exp(-gate)) * up).astype(BF)

    def down(pair):
        return jnp.dot(pair[0], WD[0], preferred_element_type=F32) + jnp.dot(
            pair[1], WD[1], preferred_element_type=F32
        )

    def decode_ffn():
        drain_recv(DX2.at[pl.ds(0, 15)], mr.at[9])
        hidden = rows_of(DX2)
        spread_decode(down([gated(hidden, core) for core in range(2)]), DY2, DR2, 10)

    def final_row():
        drain_recv(DR2.at[pl.ds(0, 15)], mr.at[10])
        FIN[t] = add_normed_row(DX2[q], DR2, 3)
        group_peers(lambda dev: remote(FIN.at[t], FIN.at[t], ms.at[11], mr.at[11], dev).start())

    def column_gated(a):
        hidden = jnp.concatenate([X2[rows, :] for rows in column_blocks(a)], axis=0)
        for core in range(2):
            ACT[core, pl.ds(mul(a, HD), HD), :] = gated(hidden, core)

    def column_down(a):
        rows = pl.ds(mul(a, HD), HD)
        result = down([ACT[0, rows, :], ACT[1, rows, :]]).astype(BF)
        for i, place in enumerate(column_blocks(a)):
            Y2[place, :] = result[32 * i : 32 * i + 32]

    mine = lax.broadcasted_iota(jnp.int32, (16, D), 0) == q

    def own_row_of(rows):
        return jnp.sum(jnp.where(mine, rows, 0.0), axis=0, keepdims=True).astype(BF)

    def fresh_out():
        own_fresh.wait()
        drain_recv(KN.at[:, pl.ds(0, 496)], mr.at[7])
        new_prompt_kv[...] = NKV[...]
        new_decode_kv[0, 0:1, :] = own_row_of(KH[...])
        new_decode_kv[0, 1:2, :] = own_row_of(DKV[1].astype(F32))

    slot_of = lax.broadcasted_iota(jnp.int32, (32, 16, HD), 0) + 32 * y
    crossing = []

    def wanted_row(yy):
        wanted = slots[32 * yy + t]
        return jnp.sum(jnp.where(slot_of == wanted, FIN[...].astype(F32), 0.0), axis=0)

    def cross_rows():
        drain_recv(FIN.at[pl.ds(0, 31)], mr.at[11])
        FD[0] = wanted_row(y)
        for i in (1, 2, 3):
            other = lax.rem(y + i, 4)
            FD[3 + i] = wanted_row(other)
            copy = pltpu.make_async_remote_copy(
                src_ref=FD.at[3 + i],
                dst_ref=FD.at[i],
                send_sem=ys.at[i - 1],
                recv_sem=yr.at[i - 1],
                device_id={"dp": other},
                device_id_type=MESH,
            )
            copy.start()
            crossing.append(copy)

    def decode_rows_out():
        result = FD[0]
        for i, copy in enumerate(crossing):
            copy.wait_recv()
            result = result + FD[1 + i]
        for j in range(HEADS):
            decode_out[:, j * HD : (j + 1) * HD] = result[j : j + 1, :].astype(BF)

    second_sum = Reduce(p, Y2, RB2, r2s, r2r, sends)
    tasks = [lambda: None, decode_ffn, fresh_out]
    order = 0
    for step in steps:
        if step is not None:
            column_gated(step)
            column_down(step)
            second_sum.first_hop(order)
            second_sum.leaves(order)
            order += 1
            if order == 4:
                second_sum.second_hop(0)
        elif tasks:
            tasks.pop(0)()
    final_row()
    second_sum.second_hop(1)
    second_sum.second_hop(2)
    second_sum.second_hop(3)
    second_sum.column_sum(1)
    second_sum.column_sum(2)
    cross_rows()
    second_sum.column_sum(3)
    second_sum.column_sum(0)
    decode_rows_out()
    out_rows = add_normed_rows(X2[own_block, :].astype(F32), second_sum.own_sum(), 3)
    FS[...] = out_rows.reshape(2, 16, D)
    swap = remote(FS.at[1 - c], PO.at[c], ws.at[5], wr.at[5], sib)
    swap.start()
    PO[c] = FS[c]

    for copy in sends + crossing + [piece]:
        copy.wait_send()
    for there in weights_there:
        there.wait_send()
    drain_send(DX.at[pl.ds(0, 15)], ms.at[0])
    drain_send(CK.at[:, pl.ds(0, 31)], ms.at[1])
    drain_send(OR.at[pl.ds(0, 31)], ms.at[2])
    drain_send(KN.at[:, pl.ds(0, 240)], ms.at[3])
    drain_send(OR.at[pl.ds(0, 31)], ms.at[4])
    drain_send(SR.at[pl.ds(0, 31)], ms.at[5])
    drain_send(SS.at[pl.ds(0, 15)], ms.at[6])
    drain_send(KN.at[:, pl.ds(0, 496)], ms.at[7])
    drain_send(DR.at[pl.ds(0, 15)], ms.at[8])
    drain_send(DX2.at[pl.ds(0, 15)], ms.at[9])
    drain_send(DR2.at[pl.ds(0, 15)], ms.at[10])
    drain_send(FIN.at[pl.ds(0, 31)], ms.at[11])
    swap.wait()
    prompt_out[...] = PO[...]


def place(*refs):
    for src, dst in zip(refs[:4], refs[4:]):
        dst[...] = src[...]


def local(
    prompt_states,
    decode_states,
    cache,
    prompt_starts,
    decode_lengths,
    decode_slots,
    w_qkv,
    w_out,
    w_gate_up,
    w_down,
    gains,
):
    freq = np.power(ROPE_BASE, -2.0 * (np.arange(HD) // 2) / HD).astype(np.float32)[None, :]
    vmem = pl.BlockSpec(memory_space=pltpu.VMEM)
    smem = pl.BlockSpec(memory_space=pltpu.SMEM)
    hbm = pl.BlockSpec(memory_space=pl.ANY)
    scratch = [
        ((512, D), BF),
        ((512, D), BF),
        ((512, D), BF),
        ((512, D), BF),
        ((480, D), BF),
        ((480, D), BF),
        ((3, 2, 64, D), BF),
        ((2, 64, D), BF),
        ((2, 2, D, FFD), BF),
        ((2, FFD, D), BF),
        ((32, CTX, D), BF),
        ((32, CTX, D), BF),
        ((2, 32, CTX, HD), BF),
        ((512, HD), BF),
        ((2, 512, HD), BF),
        ((2, 2, 16, D), BF),
        ((2, 512, FFD), BF),
        ((16, 8, HD), F32),
        ((16, 16, HD), BF),
        ((16, D), BF),
        ((2, 16, D), BF),
        ((2, 16, D), BF),
        ((32, D), F32),
        ((16, D), F32),
        ((32, HD), F32),
        ((2, 32, HD), F32),
        ((32, D), F32),
        ((2, 16, D), BF),
        ((2, 16, 8, HD), F32),
        ((32, 16, HD), BF),
        ((32, 8, HD), F32),
        ((16, 16, HD), BF),
        ((16, 16, HD), BF),
        ((16, 16, HD), BF),
        ((16, 16, HD), BF),
        ((16, 16, HD), BF),
        ((2, 16, D), BF),
        ((32, 16, HD), BF),
        ((2, 16, D), BF),
        ((7, 16, HD), F32),
        ((16, HD), F32),
        ((16, 16, HD), F32),
        ((2, 512, HD), F32),
    ]
    sems = [20, 20, 20, 20, 30, 30, 30, 30, 6, 6, 9, 4, 12, 12, 3, 3]
    outs = pl.pallas_call(
        kernel,
        out_shape=(
            jax.ShapeDtypeStruct((2, 16, D), BF),
            jax.ShapeDtypeStruct((1, D), BF),
            jax.ShapeDtypeStruct((2, 2, 16, D), BF),
            jax.ShapeDtypeStruct((1, 2, D), BF),
        ),
        in_specs=[hbm, vmem, hbm, smem, vmem, vmem, smem, hbm, hbm, hbm, hbm, vmem, vmem],
        out_specs=(vmem, vmem, vmem, vmem),
        scratch_shapes=[pltpu.VMEM(shape, dtype) for shape, dtype in scratch]
        + [pltpu.SemaphoreType.DMA((count,)) for count in sems],
        compiler_params=pltpu.CompilerParams(
            collective_id=0, has_side_effects=True, vmem_limit_bytes=60 * 1024 * 1024
        ),
        name="decoder_layer",
    )(
        prompt_states,
        decode_states,
        cache,
        prompt_starts,
        decode_lengths[None, :],
        decode_slots[None, :],
        decode_slots,
        jnp.swapaxes(w_qkv, 1, 2),
        w_out,
        w_gate_up,
        w_down,
        gains,
        jnp.asarray(freq),
    )
    placed = pl.pallas_call(
        place,
        out_shape=tuple(jax.ShapeDtypeStruct(out.shape, out.dtype) for out in outs),
        in_specs=[vmem] * 4,
        out_specs=(vmem,) * 4,
        name="place",
    )(*outs)
    return placed[0], placed[1], placed[2], jnp.swapaxes(placed[3], 0, 1)


def solution(mesh):
    in_specs = (
        P("dp", "tensor", None),
        P(("dp", "tensor"), None),
        P(None, "dp", "tensor", None),
        P(),
        P(),
        P(),
        P(None, None, "tensor"),
        P("tensor", None),
        P(None, None, "tensor"),
        P("tensor", None),
        P(),
    )
    out_specs = (
        P("dp", "tensor", None),
        P(("dp", "tensor"), None),
        P(None, "dp", "tensor", None),
        P(None, ("dp", "tensor"), None),
    )
    return jax.shard_map(local, mesh=mesh, in_specs=in_specs, out_specs=out_specs, check_vma=False)
```

```python
import jax
import jax.numpy as jnp
import numpy as np
from jax import lax
from jax.experimental import pallas as pl
from jax.experimental.pallas import tpu as pltpu
from jax.sharding import PartitionSpec as P

D = 2048
HD = 128
HEADS = 16
FFD = 256
CTX = 48
EPSILON = 1e-06
ROPE_BASE = 500000.0
MASKED_SCORE = -1e30
LOG2E = 1.4426950408889634
SCALE = HD ** (-0.5)
BF = jnp.bfloat16
F32 = jnp.float32
MESH = pl.DeviceIdType.MESH
NT = (((1,), (1,)), ((), ()))


def mul(value, factor):
    return pl.multiple_of(value * factor, factor)


def remote(src, dst, send_sem, recv_sem, dev):
    return pltpu.make_async_remote_copy(
        src_ref=src,
        dst_ref=dst,
        send_sem=send_sem,
        recv_sem=recv_sem,
        device_id={"tensor": dev},
        device_id_type=MESH,
    )


class Plane:
    def __init__(self):
        self.y = lax.axis_index("dp")
        self.t = lax.axis_index("tensor")
        self.c = lax.rem(self.t, 2)
        self.q = lax.div(self.t, 2)
        x = lax.rem(self.q, 4)
        z = lax.div(self.q, 4)
        self.a = x + self.c * (z - x)
        self.b = z + self.c * (x - z)
        self.sib = self.t + 1 - 2 * self.c
        self.aR, self.aO, self.aL = [lax.rem(self.a + i, 4) for i in (1, 2, 3)]
        self.bR, self.bO, self.bL = [lax.rem(self.b + i, 4) for i in (1, 2, 3)]

    def chip(self, a, b):
        return a * (1 + 3 * self.c) + b * (4 - 3 * self.c)

    def dev(self, a, b):
        return 2 * self.chip(a, b) + self.c


def block(buf, chip):
    return buf.at[pl.ds(mul(chip, 32), 32)]


def half(buf, chip, h):
    return buf.at[pl.ds(mul(chip * 2 + h, 16), 16)]


def gather_steps(p, buf, ss, rs, sends):
    def send(slot, ref, dev):
        copy = remote(ref, ref, ss.at[slot], rs.at[slot], dev)
        copy.start()
        sends.append(copy)

    def recv(slot, ref):
        remote(ref, ref, ss.at[slot], rs.at[slot], p.dev(p.aR, p.b)).wait_recv()

    def blk(a, b):
        return block(buf, p.chip(a, b))

    def hlf(a, b, h):
        return half(buf, p.chip(a, b), h)

    a, b, aR, aL, aO, bR, bL, bO = p.a, p.b, p.aR, p.aL, p.aO, p.bR, p.bL, p.bO
    to_aR, to_aL, to_bR, to_bL = p.dev(aR, b), p.dev(aL, b), p.dev(a, bR), p.dev(a, bL)
    own = blk(a, b)
    send(0, own, to_aR)
    send(1, own, to_aL)
    send(2, own, p.dev(aO, b))
    send(4, own, to_bR)
    send(5, own, to_bL)
    yield
    recv(0, blk(aL, b))
    send(8, blk(aL, b), to_bR)
    send(9, blk(aL, b), to_bL)
    recv(1, blk(aR, b))
    send(12, blk(aR, b), to_bR)
    send(13, blk(aR, b), to_bL)
    yield
    recv(4, blk(a, bL))
    send(6, hlf(a, bL, 0), to_bR)
    recv(5, blk(a, bR))
    send(7, hlf(a, bR, 1), to_bL)
    yield
    recv(2, blk(aO, b))
    send(16, blk(aO, b), to_bR)
    send(17, blk(aO, b), to_bL)
    yield
    columns = (a, aL, aR, aO)
    for k in (1, 2, 3):
        recv(4 + 4 * k, blk(columns[k], bL))
        send(6 + 4 * k, hlf(columns[k], bL, 0), to_bR)
        recv(5 + 4 * k, blk(columns[k], bR))
        send(7 + 4 * k, hlf(columns[k], bR, 1), to_bL)
        yield
        for done in ((), (), (0,), (1, 2, 3))[k]:
            recv(6 + 4 * done, hlf(columns[done], bO, 0))
            recv(7 + 4 * done, hlf(columns[done], bO, 1))
            yield columns[done]


class Reduce:
    def __init__(self, p, buf, land, ss, rs, sends):
        self.p, self.buf, self.land, self.ss, self.rs, self.sends = p, buf, land, ss, rs, sends
        self.columns = (p.a, p.aL, p.aR, p.aO)
        self.owners = [p.dev(column, p.b) for column in self.columns]
        self.to_bR, self.to_bL = p.dev(p.a, p.bR), p.dev(p.a, p.bL)

    def place(self, slot):
        return self.land.at[pl.ds(16 * slot, 16 if slot < 24 else 32)]

    def send(self, slot, ref, dev):
        copy = remote(ref, self.place(slot), self.ss.at[slot], self.rs.at[slot], dev)
        copy.start()
        self.sends.append(copy)

    def add(self, ref, slots):
        total = ref[...].astype(F32)
        for slot in slots:
            place = self.place(slot)
            remote(place, place, self.ss.at[slot], self.rs.at[slot], self.to_bR).wait_recv()
            total = total + place[...].astype(F32)
        return total

    def half(self, k, b, h):
        return half(self.buf, self.p.chip(self.columns[k], b), h)

    def first_hop(self, k):
        self.send(6 * k + 0, self.half(k, self.p.bO, 0), self.to_bL)
        self.send(6 * k + 1, self.half(k, self.p.bO, 1), self.to_bR)

    def leaves(self, k):
        self.send(6 * k + 2, self.half(k, self.p.bL, 1), self.to_bL)
        self.send(6 * k + 3, self.half(k, self.p.bR, 0), self.to_bR)

    def second_hop(self, k):
        ref = self.half(k, self.p.bL, 0)
        ref[...] = self.add(ref, (6 * k + 0,)).astype(BF)
        self.send(6 * k + 4, ref, self.to_bL)
        ref = self.half(k, self.p.bR, 1)
        ref[...] = self.add(ref, (6 * k + 1,)).astype(BF)
        self.send(6 * k + 5, ref, self.to_bR)

    def column_sum(self, k):
        h0, h1 = self.half(k, self.p.b, 0), self.half(k, self.p.b, 1)
        h0[...] = self.add(h0, (6 * k + 3, 6 * k + 4)).astype(BF)
        h1[...] = self.add(h1, (6 * k + 2, 6 * k + 5)).astype(BF)
        if k > 0:
            self.send(22 + 2 * k, block(self.buf, self.p.chip(self.columns[k], self.p.b)), self.owners[k])

    def own_sum(self):
        return self.add(block(self.buf, self.p.chip(self.p.a, self.p.b)), (24, 26, 28))


def turn(values, cosine, sine):
    lane = lax.broadcasted_iota(jnp.int32, values.shape, 1)
    swapped = jnp.where(lane % 2 == 0, pltpu.roll(values, HD - 1, 1), pltpu.roll(values, 1, 1))
    return values * cosine + swapped * sine


def angles(positions, freq):
    turned = positions * freq
    lane = lax.broadcasted_iota(jnp.int32, turned.shape, 1)
    return jnp.cos(turned), jnp.where(lane % 2 == 0, -1.0, 1.0) * jnp.sin(turned)


def kernel(
    prompt_states,
    decode_states,
    cache,
    prompt_starts,
    lengths,
    slots_row,
    slots,
    w_qkv,
    w_out,
    w_gate_up,
    w_down,
    gains,
    freq,
    prompt_out,
    decode_out,
    new_prompt_kv,
    new_decode_kv,
    X1,
    X2,
    Y,
    Y2,
    RB1,
    RB2,
    WQ,
    WO,
    WG,
    WD,
    KD,
    VD,
    CK,
    QR,
    KN,
    NKV,
    ACT,
    SS,
    DX,
    XD,
    DQ,
    DKV,
    QH,
    KH,
    LEN,
    DCS,
    OBF,
    OB,
    SB,
    OR,
    SR,
    DY,
    DR,
    DX2,
    DY2,
    DR2,
    PO,
    FIN,
    FS,
    FD,
    WIDE,
    WIDE3,
    TURNED,
    g1s,
    g1r,
    g2s,
    g2r,
    r1s,
    r1r,
    r2s,
    r2r,
    ws,
    wr,
    wl,
    ls,
    ms,
    mr,
    ys,
    yr,
):
    p = Plane()
    y, t, c, q, sib = p.y, p.t, p.c, p.q, p.sib
    sends = []
    lanes_q = pl.ds(mul(q, HD), HD)
    own_block = pl.ds(mul(q, 32), 32)

    barrier = pltpu.get_barrier_semaphore()

    @pl.loop(1, 32)
    def _(i):
        pl.semaphore_signal(
            barrier, inc=1, device_id={"tensor": lax.rem(t + i, 32)}, device_id_type=MESH
        )

    for i in (1, 2, 3):
        pl.semaphore_signal(barrier, inc=1, device_id={"dp": lax.rem(y + i, 4)}, device_id_type=MESH)

    def plane_peers(body):
        @pl.loop(1, 16)
        def _(i):
            chip = lax.rem(q + i, 16)
            body(chip, 2 * chip + c)

    def group_peers(body, first=1, last=32):
        @pl.loop(first, last)
        def _(i):
            body(lax.rem(t + i, 32))

    def drain_recv(ref, sem):
        remote(ref, ref, sem, sem, sib).wait_recv()

    def drain_send(ref, sem):
        remote(ref, ref, sem, sem, sib).wait_send()

    def local_copy(src, dst, sem):
        copy = pltpu.make_async_copy(src, dst, sem)
        copy.start()
        return copy

    piece_here = local_copy(prompt_states.at[c], half(X1, q, c), wl.at[0])
    weight_pairs = (
        (w_qkv, WQ.at[:, c]),
        (w_out, WO.at[c]),
        (w_gate_up, WG.at[c]),
        (w_down, WD.at[c]),
    )
    weights_here = [local_copy(src, dst, wl.at[1 + i]) for i, (src, dst) in enumerate(weight_pairs)]

    def cache_slice(dev):
        return cache.at[:, lax.rem(dev, 2), :, pl.ds(mul(lax.div(dev, 2), HD), HD)]

    own_cache = local_copy(cache_slice(t), CK.at[:, t], wl.at[5])

    for j in range(HEADS):
        WIDE[pl.ds(j, 1), :] = decode_states[:, j * HD : (j + 1) * HD].astype(F32)
    DX[q] = WIDE[0:16, :].astype(BF)

    slot_row = lax.broadcasted_iota(jnp.int32, (32, HD), 0)
    slot_id = 32 * y + 2 * (slot_row % 16) + slot_row // 16
    matched = jnp.where(slots_row[...] == slot_id, lengths[...].astype(F32), 0.0)
    LEN[...] = jnp.broadcast_to(jnp.sum(matched, axis=1, keepdims=True), (32, HD))
    cosine, sine = angles(LEN[...], freq[...])
    DCS[0] = cosine
    DCS[1] = sine

    pl.semaphore_wait(barrier, 34)

    piece = remote(prompt_states.at[1 - c], half(X1, q, c), ws.at[0], wr.at[0], sib)
    piece.start()
    plane_peers(lambda chip, dev: remote(DX.at[q], DX.at[q], ms.at[0], mr.at[0], dev).start())
    weights_there = []
    for i, (src, dst) in enumerate(weight_pairs):
        weights_there.append(remote(src, dst, ws.at[1 + i], wr.at[1 + i], sib))
    weights_there[0].start()
    loads = [
        local_copy(
            cache.at[kv, pl.ds(2 + 16 * part, 16)], dst.at[pl.ds(16 * part, 16)], ls.at[2 * kv + part]
        )
        for part in range(2)
        for kv, dst in ((0, KD), (1, VD))
    ]
    for i in (1, 2, 3):
        weights_there[i].start()

    def weight_here(i):
        weights_here[i].wait()
        weights_there[i].wait_recv()

    def send_cache(first, last):
        group_peers(
            lambda dev: remote(cache_slice(dev), CK.at[:, t], ms.at[1], mr.at[1], dev).start(),
            first,
            last,
        )

    send_cache(1, 14)
    piece_here.wait()
    piece.wait_recv()
    steps = gather_steps(p, X1, g1s, g1r, sends)
    next(steps)

    def rows_of(landed):
        WIDE3[...] = landed[...].astype(F32)
        return jnp.concatenate([WIDE3[:, j, :] for j in range(HEADS)], axis=1).astype(BF)

    def project(rows):
        return lax.dot_general(rows, WQ[...].reshape(3 * HD, D), NT, preferred_element_type=F32)

    next(steps)
    next(steps)
    drain_recv(DX.at[pl.ds(0, 15)], mr.at[0])
    XD[...] = rows_of(DX)
    weight_here(0)
    dec = project(XD[...]).astype(BF)
    DQ[c, :, lanes_q] = dec[:, :HD]
    DKV[0, :, lanes_q] = dec[:, HD : 2 * HD]
    DKV[1, :, lanes_q] = dec[:, 2 * HD :]
    q_own = DQ.at[c, :, lanes_q]
    kv_own = DKV.at[:, :, lanes_q]
    group_peers(lambda dev: remote(q_own, q_own, ms.at[2], mr.at[2], dev).start())
    plane_peers(lambda chip, dev: remote(kv_own, kv_own, ms.at[3], mr.at[3], dev).start())
    next(steps)

    def normed(raw, gain_row, first):
        scale = lax.rsqrt(jnp.mean(raw * raw, axis=1, keepdims=True) + EPSILON)
        rows = raw.shape[0]
        cos_part, sin_part = DCS[0, pl.ds(first, rows), :], DCS[1, pl.ds(first, rows), :]
        parts = []
        for j in range(HEADS):
            lanes = slice(j * HD, (j + 1) * HD)
            scaled = raw[:, lanes] * scale * gains[gain_row : gain_row + 1, lanes]
            parts.append(turn(scaled, cos_part, sin_part).astype(BF).astype(F32))
        return parts

    def decode_norms():
        drain_recv(OR.at[pl.ds(0, 31)], mr.at[2])
        drain_recv(KN.at[:, pl.ds(0, 240)], mr.at[3])
        for plane in range(2):
            for j, part in enumerate(normed(DQ[plane].astype(F32), 0, 16 * plane)):
                QH[16 * plane : 16 * plane + 16, j * HD : (j + 1) * HD] = part
        for j, part in enumerate(normed(DKV[0].astype(F32), 1, mul(c, 16))):
            KH[:, j * HD : (j + 1) * HD] = part
        for load in loads:
            load.wait()

    own_lane = lax.broadcasted_iota(jnp.int32, (HEADS, D), 1) // HD
    own_row = lax.broadcasted_iota(jnp.int32, (HEADS, D), 0)
    own_head = own_lane == own_row
    spot = (lax.broadcasted_iota(jnp.int32, (HEADS, CTX), 1) + CTX * t).astype(F32)
    stat_lane = lax.broadcasted_iota(jnp.int32, (HEADS, HD), 1)

    def decode_slots_at(r):
        for plane in range(2):
            tops, totals = [], []
            for upper in range(2):
                row = 8 * upper + r
                index = 16 * plane + row
                slot = 2 * row + plane
                spread = jnp.where(own_head, QH[pl.ds(index, 1), :], 0.0).astype(BF)
                scores = lax.dot_general(spread, KD[slot], NT, preferred_element_type=F32)
                live = spot < LEN[pl.ds(index, 1), :CTX]
                scores = jnp.where(live, scores * SCALE, MASKED_SCORE)
                top = jnp.max(scores, axis=1, keepdims=True)
                probs = jnp.where(live, jnp.exp(scores - top), 0.0)
                tops.append(top)
                totals.append(jnp.sum(probs, axis=1, keepdims=True))
                mixed = jnp.dot(probs.astype(BF), VD[slot], preferred_element_type=F32)
                OBF[pl.ds(index, 1), :] = jnp.sum(
                    jnp.where(own_head, mixed, 0.0), axis=0, keepdims=True
                )
            SB[plane, :, r, :] = jnp.where(
                stat_lane < 64,
                jnp.where(stat_lane < 32, tops[0], totals[0]),
                jnp.where(stat_lane < 96, tops[1], totals[1]),
            )

    stat_row = lax.broadcasted_iota(jnp.int32, (8, HD), 0)
    SS[q] = jnp.zeros((8, HD), F32)

    def column_blocks(a):
        return [pl.ds(mul(p.chip(a, i), 32), 32) for i in range(4)]

    def row_sums(values):
        total = jnp.sum(values * values, axis=1, keepdims=True)
        return jnp.broadcast_to(total, (HD, HD)).T[0:8, :]

    def column_project(a):
        rows = pl.ds(mul(a, HD), HD)
        got = project(jnp.concatenate([X1[place, :] for place in column_blocks(a)], axis=0)).astype(BF)
        QR[rows, :] = got[:, :HD]
        KN[0, rows, :] = got[:, HD : 2 * HD]
        KN[1, rows, :] = got[:, 2 * HD :]
        query_sum = row_sums(got[:, :HD].astype(F32))
        key_sum = row_sums(got[:, HD : 2 * HD].astype(F32))
        SS[q] = jnp.where(
            stat_row == a, query_sum, jnp.where(stat_row == 4 + a, key_sum, SS[q])
        )

    next(steps)
    next(steps)
    send_cache(14, 32)
    column_project(next(steps))
    decode_norms()
    next(steps)
    for r, column in enumerate(steps):
        column_project(column)
        if r < 2:
            decode_slots_at(r)
    plane_peers(lambda chip, dev: remote(SS.at[q], SS.at[q], ms.at[6], mr.at[6], dev).start())
    for r in range(2, 8):
        decode_slots_at(r)

    OB[0] = OBF[0:16, :].astype(BF)
    OB[1] = OBF[16:32, :].astype(BF)

    def mixed_slice(dev):
        return OB.at[lax.rem(dev, 2), :, pl.ds(mul(lax.div(dev, 2), HD), HD)]

    def stat_slice(dev):
        return SB.at[lax.rem(dev, 2), lax.div(dev, 2)]

    own_mixed = local_copy(mixed_slice(t), OR.at[t], wl.at[6])
    own_stat = local_copy(stat_slice(t), SR.at[t], wl.at[7])

    def send_partial(dev):
        remote(mixed_slice(dev), OR.at[t], ms.at[4], mr.at[4], dev).start()
        remote(stat_slice(dev), SR.at[t], ms.at[5], mr.at[5], dev).start()

    group_peers(send_partial)

    start = prompt_starts[2 * y + c]

    def offsets_of(index):
        chips = (index // HD) * (1 + 3 * c) + (index // 32 % 4) * (4 - 3 * c)
        return chips * 32 + index % 32

    for i in range(4):
        rows = slice(i * HD, (i + 1) * HD)
        offset = offsets_of(lax.broadcasted_iota(jnp.int32, (HD, HD), 0) + i * HD)
        cosine, sine = angles((offset + start).astype(F32), freq[...])
        for kind in range(2):
            raw = (QR[rows, :] if kind == 0 else KN[0, rows, :]).astype(F32)
            TURNED[kind, rows, :] = turn(raw * gains[kind : kind + 1, lanes_q], cosine, sine)
    drain_recv(SS.at[pl.ds(0, 15)], mr.at[6])
    scales = lax.rsqrt(jnp.sum(SS[...], axis=0) * (1.0 / D) + EPSILON)
    for i in range(4):
        rows = slice(i * HD, (i + 1) * HD)
        for kind in range(2):
            column = jnp.broadcast_to(scales[4 * kind + i : 4 * kind + i + 1, :], (HD, HD)).T
            turned = (TURNED[kind, rows, :] * column).astype(BF)
            if kind == 0:
                QR[rows, :] = turned
            else:
                KN[0, rows, :] = turned

    def fresh_slice(dev):
        chip = lax.div(dev, 2)
        low, high = lax.rem(chip, 4), lax.div(chip, 4)
        a, b = low + c * (high - low), high + c * (low - high)
        return KN.at[:, pl.ds(mul(8 * a + 2 * b + lax.rem(dev, 2), 16), 16), :]

    landing = NKV.at[:, c, :, lanes_q]
    own_fresh = local_copy(fresh_slice(t), landing, wl.at[8])
    group_peers(lambda dev: remote(fresh_slice(dev), landing, ms.at[7], mr.at[7], dev).start())

    own_mixed.wait()
    own_stat.wait()
    drain_recv(OR.at[pl.ds(0, 31)], mr.at[4])
    drain_recv(SR.at[pl.ds(0, 31)], mr.at[5])

    def stat(lane):
        parts = [
            jnp.broadcast_to(SR[:, :, lane + 64 * k : lane + 64 * k + 1], (32, 8, HD)) for k in (0, 1)
        ]
        return jnp.concatenate(parts, axis=1)

    tops, totals = stat(0), stat(32)
    own_rows = pl.ds(mul(c, 16), 16)
    own_score = (
        jnp.sum(QH[own_rows, lanes_q] * KH[:, lanes_q], axis=1, keepdims=True) * SCALE
    )
    highest = jnp.maximum(jnp.max(tops, axis=0), own_score)
    factors = jnp.exp(tops - highest[None])
    own_weight = jnp.exp(own_score - highest)
    total = jnp.sum(totals * factors, axis=0) + own_weight
    mixed = jnp.sum(OR[...].astype(F32) * factors, axis=0)
    mixed = mixed + own_weight.astype(BF).astype(F32) * DKV[1, :, lanes_q].astype(F32)
    attended_rows = (mixed / total).astype(BF)

    weight_here(1)

    def spread_decode(tail, staged, landed, index):
        for j in range(HEADS):
            WIDE3[:, j, :] = tail[:, j * HD : (j + 1) * HD]
        staged[...] = WIDE3[...].astype(BF)
        landed[q] = staged[q]
        plane_peers(
            lambda chip, dev: remote(
                staged.at[chip], landed.at[q], ms.at[index], mr.at[index], dev
            ).start()
        )

    def row_of(gain):
        parts = [gains[gain : gain + 1, j * HD : (j + 1) * HD] for j in range(HEADS)]
        return jnp.concatenate(parts, axis=0)

    def add_normed_rows(base, total, gain):
        scale = lax.rsqrt(jnp.mean(total * total, axis=1, keepdims=True) + EPSILON)
        return (base + total * scale * gains[gain : gain + 1, :]).astype(BF)

    def add_normed_row(base, landed, gain):
        total = jnp.sum(landed[...].astype(F32), axis=0)
        square = jnp.sum(total * total, axis=1, keepdims=True)
        mean = jnp.sum(square, axis=0, keepdims=True) * (1.0 / D)
        scale = lax.rsqrt(mean + EPSILON)
        return (base.astype(F32) + total * scale * row_of(gain)).astype(BF)

    w_head = WO[...].reshape(HD, D)
    spread_decode(jnp.dot(attended_rows, w_head, preferred_element_type=F32), DY, DR, 8)

    own_cache.wait()
    drain_recv(CK.at[:, pl.ds(0, 31)], mr.at[1])
    cached_spot = lax.broadcasted_iota(jnp.int32, (1, 32 * CTX), 1)
    cached_bias = jnp.where(cached_spot < start, 0.0, MASKED_SCORE)

    def column_attend(a):
        query = QR[pl.ds(mul(a, HD), HD), :]
        cached_keys = CK[0].reshape(32 * CTX, HD)
        cached_values = CK[1].reshape(32 * CTX, HD)
        fresh = lax.dot_general(query, KN[0], NT, preferred_element_type=F32)
        cached = lax.dot_general(query, cached_keys, NT, preferred_element_type=F32)
        column = offsets_of(lax.broadcasted_iota(jnp.int32, (1, 512), 1))
        row = offsets_of(lax.broadcasted_iota(jnp.int32, (HD, 1), 0) + a * HD)
        fresh = jnp.where(column <= row, fresh, MASKED_SCORE)
        cached = cached + cached_bias
        top = jnp.maximum(
            jnp.max(fresh, axis=1, keepdims=True), jnp.max(cached, axis=1, keepdims=True)
        )
        fresh = jnp.exp2((fresh - top) * (SCALE * LOG2E))
        cached = jnp.exp2((cached - top) * (SCALE * LOG2E))
        total = jnp.sum(fresh, axis=1, keepdims=True) + jnp.sum(cached, axis=1, keepdims=True)
        mixed = jnp.dot(fresh.astype(BF), KN[1], preferred_element_type=F32)
        mixed = mixed + jnp.dot(cached.astype(BF), cached_values, preferred_element_type=F32)
        result = jnp.dot(
            (mixed / total).astype(BF), w_head, preferred_element_type=F32
        ).astype(BF)
        for i, place in enumerate(column_blocks(a)):
            Y[place, :] = result[32 * i : 32 * i + 32]

    def hidden_row():
        drain_recv(DR.at[pl.ds(0, 15)], mr.at[8])
        DX2[q] = add_normed_row(DX[q], DR, 2)
        plane_peers(lambda chip, dev: remote(DX2.at[q], DX2.at[q], ms.at[9], mr.at[9], dev).start())

    first_sum = Reduce(p, Y, RB1, r1s, r1r, sends)
    for k in (3, 1, 2, 0):
        column_attend(first_sum.columns[k])
        first_sum.first_hop(k)
        first_sum.leaves(k)
        if k == 2:
            first_sum.second_hop(3)
    first_sum.second_hop(1)
    first_sum.column_sum(3)
    first_sum.second_hop(2)
    first_sum.column_sum(1)
    first_sum.second_hop(0)
    first_sum.column_sum(2)
    first_sum.column_sum(0)
    hidden_row()
    X2[own_block, :] = add_normed_rows(
        X1[own_block, :].astype(F32), first_sum.own_sum(), 2
    )
    steps = gather_steps(p, X2, g2s, g2r, sends)
    next(steps)

    weight_here(2)
    weight_here(3)

    def gated(hidden, core):
        gate = jnp.dot(hidden, WG[core, 0], preferred_element_type=F32)
        up = jnp.dot(hidden, WG[core, 1], preferred_element_type=F32)
        return (gate / (1.0 + jnp.exp(-gate)) * up).astype(BF)

    def down(pair):
        return jnp.dot(pair[0], WD[0], preferred_element_type=F32) + jnp.dot(
            pair[1], WD[1], preferred_element_type=F32
        )

    def decode_ffn():
        drain_recv(DX2.at[pl.ds(0, 15)], mr.at[9])
        hidden = rows_of(DX2)
        spread_decode(down([gated(hidden, core) for core in range(2)]), DY2, DR2, 10)

    def final_row():
        drain_recv(DR2.at[pl.ds(0, 15)], mr.at[10])
        FIN[t] = add_normed_row(DX2[q], DR2, 3)
        group_peers(lambda dev: remote(FIN.at[t], FIN.at[t], ms.at[11], mr.at[11], dev).start())

    def column_gated(a):
        hidden = jnp.concatenate([X2[rows, :] for rows in column_blocks(a)], axis=0)
        for core in range(2):
            ACT[core, pl.ds(mul(a, HD), HD), :] = gated(hidden, core)

    def column_down(a):
        rows = pl.ds(mul(a, HD), HD)
        result = down([ACT[0, rows, :], ACT[1, rows, :]]).astype(BF)
        for i, place in enumerate(column_blocks(a)):
            Y2[place, :] = result[32 * i : 32 * i + 32]

    mine = lax.broadcasted_iota(jnp.int32, (16, D), 0) == q

    def own_row_of(rows):
        return jnp.sum(jnp.where(mine, rows, 0.0), axis=0, keepdims=True).astype(BF)

    def fresh_out():
        own_fresh.wait()
        drain_recv(KN.at[:, pl.ds(0, 496)], mr.at[7])
        new_prompt_kv[...] = NKV[...]
        new_decode_kv[0, 0:1, :] = own_row_of(KH[...])
        new_decode_kv[0, 1:2, :] = own_row_of(DKV[1].astype(F32))

    slot_of = lax.broadcasted_iota(jnp.int32, (32, 16, HD), 0) + 32 * y
    crossing = []

    def wanted_row(yy):
        wanted = slots[32 * yy + t]
        return jnp.sum(jnp.where(slot_of == wanted, FIN[...].astype(F32), 0.0), axis=0)

    def cross_rows():
        drain_recv(FIN.at[pl.ds(0, 31)], mr.at[11])
        FD[0] = wanted_row(y)
        for i in (1, 2, 3):
            other = lax.rem(y + i, 4)
            FD[3 + i] = wanted_row(other)
            copy = pltpu.make_async_remote_copy(
                src_ref=FD.at[3 + i],
                dst_ref=FD.at[i],
                send_sem=ys.at[i - 1],
                recv_sem=yr.at[i - 1],
                device_id={"dp": other},
                device_id_type=MESH,
            )
            copy.start()
            crossing.append(copy)

    def decode_rows_out():
        result = FD[0]
        for i, copy in enumerate(crossing):
            copy.wait_recv()
            result = result + FD[1 + i]
        for j in range(HEADS):
            decode_out[:, j * HD : (j + 1) * HD] = result[j : j + 1, :].astype(BF)

    second_sum = Reduce(p, Y2, RB2, r2s, r2r, sends)
    tasks = [lambda: None, decode_ffn, fresh_out]
    order = 0
    for step in steps:
        if step is not None:
            column_gated(step)
            column_down(step)
            second_sum.first_hop(order)
            second_sum.leaves(order)
            order += 1
            if order == 4:
                second_sum.second_hop(0)
        elif tasks:
            tasks.pop(0)()
    final_row()
    second_sum.second_hop(1)
    second_sum.second_hop(2)
    second_sum.second_hop(3)
    second_sum.column_sum(1)
    second_sum.column_sum(2)
    cross_rows()
    second_sum.column_sum(3)
    second_sum.column_sum(0)
    decode_rows_out()
    out_rows = add_normed_rows(X2[own_block, :].astype(F32), second_sum.own_sum(), 3)
    FS[...] = out_rows.reshape(2, 16, D)
    swap = remote(FS.at[1 - c], PO.at[c], ws.at[5], wr.at[5], sib)
    swap.start()
    PO[c] = FS[c]

    for copy in sends + crossing + [piece]:
        copy.wait_send()
    for there in weights_there:
        there.wait_send()
    drain_send(DX.at[pl.ds(0, 15)], ms.at[0])
    drain_send(CK.at[:, pl.ds(0, 31)], ms.at[1])
    drain_send(OR.at[pl.ds(0, 31)], ms.at[2])
    drain_send(KN.at[:, pl.ds(0, 240)], ms.at[3])
    drain_send(OR.at[pl.ds(0, 31)], ms.at[4])
    drain_send(SR.at[pl.ds(0, 31)], ms.at[5])
    drain_send(SS.at[pl.ds(0, 15)], ms.at[6])
    drain_send(KN.at[:, pl.ds(0, 496)], ms.at[7])
    drain_send(DR.at[pl.ds(0, 15)], ms.at[8])
    drain_send(DX2.at[pl.ds(0, 15)], ms.at[9])
    drain_send(DR2.at[pl.ds(0, 15)], ms.at[10])
    drain_send(FIN.at[pl.ds(0, 31)], ms.at[11])
    swap.wait()
    prompt_out[...] = PO[...]


def place(*refs):
    for src, dst in zip(refs[:4], refs[4:]):
        dst[...] = src[...]


def local(
    prompt_states,
    decode_states,
    cache,
    prompt_starts,
    decode_lengths,
    decode_slots,
    w_qkv,
    w_out,
    w_gate_up,
    w_down,
    gains,
):
    freq = np.power(ROPE_BASE, -2.0 * (np.arange(HD) // 2) / HD).astype(np.float32)[None, :]
    vmem = pl.BlockSpec(memory_space=pltpu.VMEM)
    smem = pl.BlockSpec(memory_space=pltpu.SMEM)
    hbm = pl.BlockSpec(memory_space=pl.ANY)
    scratch = [
        ((512, D), BF),
        ((512, D), BF),
        ((512, D), BF),
        ((512, D), BF),
        ((480, D), BF),
        ((480, D), BF),
        ((3, 2, 64, D), BF),
        ((2, 64, D), BF),
        ((2, 2, D, FFD), BF),
        ((2, FFD, D), BF),
        ((32, CTX, D), BF),
        ((32, CTX, D), BF),
        ((2, 32, CTX, HD), BF),
        ((512, HD), BF),
        ((2, 512, HD), BF),
        ((2, 2, 16, D), BF),
        ((2, 512, FFD), BF),
        ((16, 8, HD), F32),
        ((16, 16, HD), BF),
        ((16, D), BF),
        ((2, 16, D), BF),
        ((2, 16, D), BF),
        ((32, D), F32),
        ((16, D), F32),
        ((32, HD), F32),
        ((2, 32, HD), F32),
        ((32, D), F32),
        ((2, 16, D), BF),
        ((2, 16, 8, HD), F32),
        ((32, 16, HD), BF),
        ((32, 8, HD), F32),
        ((16, 16, HD), BF),
        ((16, 16, HD), BF),
        ((16, 16, HD), BF),
        ((16, 16, HD), BF),
        ((16, 16, HD), BF),
        ((2, 16, D), BF),
        ((32, 16, HD), BF),
        ((2, 16, D), BF),
        ((7, 16, HD), F32),
        ((16, HD), F32),
        ((16, 16, HD), F32),
        ((2, 512, HD), F32),
    ]
    sems = [20, 20, 20, 20, 30, 30, 30, 30, 6, 6, 9, 4, 12, 12, 3, 3]
    outs = pl.pallas_call(
        kernel,
        out_shape=(
            jax.ShapeDtypeStruct((2, 16, D), BF),
            jax.ShapeDtypeStruct((1, D), BF),
            jax.ShapeDtypeStruct((2, 2, 16, D), BF),
            jax.ShapeDtypeStruct((1, 2, D), BF),
        ),
        in_specs=[hbm, vmem, hbm, smem, vmem, vmem, smem, hbm, hbm, hbm, hbm, vmem, vmem],
        out_specs=(vmem, vmem, vmem, vmem),
        scratch_shapes=[pltpu.VMEM(shape, dtype) for shape, dtype in scratch]
        + [pltpu.SemaphoreType.DMA((count,)) for count in sems],
        compiler_params=pltpu.CompilerParams(
            collective_id=0, has_side_effects=True, vmem_limit_bytes=60 * 1024 * 1024
        ),
        name="decoder_layer",
    )(
        prompt_states,
        decode_states,
        cache,
        prompt_starts,
        decode_lengths[None, :],
        decode_slots[None, :],
        decode_slots,
        jnp.swapaxes(w_qkv, 1, 2),
        w_out,
        w_gate_up,
        w_down,
        gains,
        jnp.asarray(freq),
    )
    placed = pl.pallas_call(
        place,
        out_shape=tuple(jax.ShapeDtypeStruct(out.shape, out.dtype) for out in outs),
        in_specs=[vmem] * 4,
        out_specs=(vmem,) * 4,
        name="place",
    )(*outs)
    return placed[0], placed[1], placed[2], jnp.swapaxes(placed[3], 0, 1)


def solution(mesh):
    in_specs = (
        P("dp", "tensor", None),
        P(("dp", "tensor"), None),
        P(None, "dp", "tensor", None),
        P(),
        P(),
        P(),
        P(None, None, "tensor"),
        P("tensor", None),
        P(None, None, "tensor"),
        P("tensor", None),
        P(),
    )
    out_specs = (
        P("dp", "tensor", None),
        P(("dp", "tensor"), None),
        P(None, "dp", "tensor", None),
        P(None, ("dp", "tensor"), None),
    )
    return jax.shard_map(local, mesh=mesh, in_specs=in_specs, out_specs=out_specs, check_vma=False)
```
